32 devices in a mesh: section: 4 (over x, core), tp: 8 (over z, y).
Axes of the slice: x: 2, y: 2, z: 4, core: 2. Of those that a mesh axis runs over, the one named last changes fastest.
Arguments:
- hidden: bfloat16 [1024, 8192], P(('section', 'tp')), may hold values from -6 to 6
- norm_gain: float32 [4, 8192], P('section'), may hold values from 0.5 to 1.5
- w_query: bfloat16 [4, 8192, 8192], P('section', None, 'tp'), may hold values from -0.125 to 0.125
- w_keyval: bfloat16 [4, 8192, 2048], P('section', None, 'tp'), may hold values from -0.0625 to 0.0625
- w_out: bfloat16 [4, 8192, 8192], P('section', 'tp'), may hold values from -0.25 to 0.25
- kv_pool: bfloat16 [4, 32, 128, 2048], P('section', 'tp'), may hold values from -70 to 70
- page_table: int32 [4, 32], P('section'), may hold values from 0 to 31, as said below
- prefix_len: int32 [4, 4], P('section'), may hold values from 1 to 1024, 2560 in all within a row
- decode_place: int32 [4, 32], P('section'), may hold values from 0 to 31, each once within a row
Outputs:
- handed: bfloat16 [1024, 8192], P(('section', 'tp'))
- decode_cache: bfloat16 [4, 32, 64, 256], P('section', 'tp')
The draws below stay inside these ranges and needn't reach their ends.
Inputs may be any that keep to these rules, and one draw needn't show every extreme that they name: `page_table`: every page of a section's pool appears once in its page table, and of the pages k * 4 to k * 4 + 3 exactly 1 stand in each request's list. `prefix_len`: some request of every section has exactly 1024 prefix tokens. `decode_place`: every slot appears once for each section.
All inputs are finite; a program needn't handle non-finite values.
Results may differ from the reference program's by a relative error of at most 0.024.
The reference program's roundings to bfloat16 on the way (of `normed`, `query`, `keyval`, `weights`, `attended` and `block`) count: a program that leaves them out, or rounds other values in their place, can miss the bound.
Values may be sent and summed in bfloat16 or wider, within the bound.
A program may use at most 128 MiB of HBM per device.

```python
import math
import jax
import jax.numpy as jnp
import numpy as np
from jax import lax

D = 8192
H = 64
KVH = 8
HD = 128
PAGE = 128
REQ = 4
NEW = 64
POOL_DEV = 4
MAXPAGES = 8
TOTAL_ROWS = 1024
N_SECTION = 4
N_TP = 8


def draw_kv_pool(key, part):
    key = jax.random.fold_in(key, 11)
    shape = (N_SECTION, POOL_DEV * N_TP, PAGE, 2 * KVH * HD)
    first = jax.random.fold_in(key, 1)
    values = jnp.clip(jax.random.normal(first, shape, jnp.float32), -6.0, 6.0)
    return values.astype(jnp.bfloat16)


def draw_page_table(key, part):
    key = jax.random.fold_in(key, 23)
    per_request = POOL_DEV // REQ
    listed = POOL_DEV * N_TP // REQ

    def one_section(section_key):
        owner_key = jax.random.fold_in(section_key, 1)
        list_key = jax.random.fold_in(section_key, 2)
        local_order = jax.vmap(lambda k: jax.random.permutation(k, POOL_DEV))(jax.random.split(owner_key, N_TP))
        items = jax.vmap(lambda k: jax.random.permutation(k, listed))(jax.random.split(list_key, REQ))
        owners = items // per_request
        within = items % per_request
        request_ids = jnp.arange(REQ, dtype=jnp.int32)[:, None]
        local_page = local_order[owners, request_ids * per_request + within]
        return (owners * POOL_DEV + local_page).reshape(-1).astype(jnp.int32)
    return jax.vmap(one_section)(jax.random.split(key, N_SECTION))


def levels(stream_key, shape, cuts, smallest, high):
    level, own = 1.0, jax.random.fold_in(stream_key, 6)
    for position, parts in cuts:
        heights = jnp.exp(jax.random.uniform(jax.random.fold_in(own, position), (parts,), jnp.float32, smallest / len(cuts), high / len(cuts)))
        level = level * jnp.repeat(heights, shape[position] // parts).reshape([-1 if axis == position else 1 for axis in range(len(shape))])
    return level


def profile(count, total, bound, skew):
    weights = [(1 << 20) // math.isqrt(grade ** skew) + 1 for grade in range(2, count + 1)]
    surplus, given = total - bound - (count - 1), [1] * (count - 1)
    while surplus > 0:
        candidates = [i for i in range(count - 1) if given[i] < bound]
        mass, remaining = sum([weights[i] for i in candidates]), surplus
        for i in candidates:
            extra = min(bound - given[i], max(1, remaining * weights[i] // mass), surplus)
            given[i] = given[i] + extra
            surplus = surplus - extra
    return np.array([bound] + given)


def uneven(stream_key, number_of, total, limit, skew):
    if number_of == 2:
        one = jax.random.randint(stream_key, (), max(1, total - limit), min(limit, total - 1) + 1)
        return jnp.stack([one, total - one])
    lengths = jnp.asarray(profile(number_of, total, limit, skew), jnp.int32)
    pairs = (number_of - 1) // 2
    giver, receiver = lengths[1:1 + 2 * pairs:2], lengths[2:2 + 2 * pairs:2]
    room = jnp.minimum(giver - 1, limit - receiver)
    passed = jax.random.randint(jax.random.fold_in(stream_key, 1), (pairs,), 0, 1 << 20) % (room + 1)
    lengths = lengths.at[1:1 + 2 * pairs:2].set(giver - passed).at[2:2 + 2 * pairs:2].set(receiver + passed)
    return lengths[jax.random.permutation(jax.random.fold_in(stream_key, 2), number_of)]


def bell_draw(key, extent, scale, reach, cuts=(), kind=jnp.bfloat16):
    values = scale * jax.random.normal(key, extent, jnp.float32)
    if cuts:
        values = values * levels(key, extent, cuts, -0.22, 0.18)
    return jnp.clip(values, -reach, reach).astype(kind)


def setup_inputs(seed: int = 0) -> dict:
    key_of = jax.random.split(jax.random.key(seed), 10)
    return {
        "hidden": bell_draw(key_of[0], (TOTAL_ROWS, D), 1.0, 6.0, ((0, 32),)),
        "norm_gain": jnp.clip(1.0 + 0.1 * jax.random.normal(key_of[1], (N_SECTION, D), jnp.float32), 0.5, 1.5),
        "w_query": bell_draw(key_of[2], (N_SECTION, D, H * HD), (D // 4) ** -0.5, 0.125, ((0, 4), (2, 8))),
        "w_keyval": bell_draw(key_of[3], (N_SECTION, D, 2 * KVH * HD), D ** -0.5, 0.0625, ((0, 4), (2, 8))),
        "w_out": bell_draw(key_of[4], (N_SECTION, H * HD, D), (H * HD // 16) ** -0.5, 0.25, ((0, 4), (1, 8))),
        "kv_pool": draw_kv_pool(jax.random.fold_in(key_of[9], 71), 0),
        "page_table": draw_page_table(jax.random.fold_in(key_of[9], 71), 0),
        "prefix_len": jax.vmap(lambda own: uneven(own, REQ, REQ * MAXPAGES * PAGE * 5 // 8, MAXPAGES * PAGE, 2))(jax.random.split(key_of[7], N_SECTION)).reshape((N_SECTION, REQ)).astype(jnp.int32),
        "decode_place": jax.vmap(lambda own: jax.random.permutation(own, REQ * KVH))(jax.random.split(key_of[8], N_SECTION)).reshape((N_SECTION, REQ * KVH)).astype(jnp.int32),
    }


rope_theta = 500000.0

def rotate(values, positions, dims, apply, head_size):
    rows = values.shape[0]
    cols = values.shape[1]
    inverse = jnp.power(rope_theta, -(dims // 2 * 2).astype(jnp.float32) / head_size)
    angle = positions[:, None].astype(jnp.float32) * inverse[None, :]
    cosine = jnp.cos(angle)[:, 0::2]
    sine = jnp.sin(angle)[:, 0::2]
    pairs = values.reshape(rows, cols // 2, 2)
    even = pairs[:, :, 0]
    odd = pairs[:, :, 1]
    turned = jnp.stack([even * cosine - odd * sine, even * sine + odd * cosine], axis=-1).reshape(rows, cols)
    return jnp.where(apply[None, :], turned, values)

def layer(rows_in, gain, wq, wkv, wo, pool, table, lens, place):
    maxpages = table.shape[0] // REQ
    prefix = maxpages * PAGE
    group = H // KVH
    xf = rows_in.astype(jnp.float32)
    meansq = lax.optimization_barrier(jnp.mean(xf * xf, axis=-1, keepdims=True))
    normed = (xf * lax.rsqrt(meansq + 1e-05) * gain[None, :]).astype(jnp.bfloat16)
    query_raw = jnp.dot(normed, wq, preferred_element_type=jnp.float32)
    keyval_raw = jnp.dot(normed, wkv, preferred_element_type=jnp.float32)
    positions = (lens[:, None] + jnp.arange(NEW, dtype=jnp.int32)[None, :]).reshape(-1)
    qcols = jnp.arange(H * HD, dtype=jnp.int32)
    query = rotate(query_raw, positions, qcols % HD, qcols >= 0, HD).astype(jnp.bfloat16)
    kcols = jnp.arange(2 * KVH * HD, dtype=jnp.int32)
    keyval = rotate(keyval_raw, positions, kcols % HD, kcols // HD % 2 == 0, HD).astype(jnp.bfloat16)
    pages = pool[table.reshape(REQ, maxpages)].reshape(REQ, prefix, KVH, 2 * HD)
    fresh = keyval.reshape(REQ, NEW, KVH, 2 * HD)
    keys = jnp.concatenate([pages, fresh], axis=1)
    kpos = jnp.arange(prefix + NEW, dtype=jnp.int32)
    npos = jnp.arange(NEW, dtype=jnp.int32)
    visible = jnp.where(kpos[None, None, :] < prefix, kpos[None, None, :] < lens[:, None, None], kpos[None, None, :] - prefix <= npos[None, :, None])
    visible = visible[:, None, :, :]
    qheads = query.reshape(REQ, NEW, KVH, group, HD).transpose(2, 0, 1, 3, 4)
    kheads = keys.transpose(2, 0, 1, 3)

    def one_head(pair):
        qh, kh = pair
        scores = jnp.einsum('rngd,rkd->rgnk', qh.astype(jnp.float32), kh[:, :, :HD].astype(jnp.float32)) * HD ** (-0.5)
        top = lax.optimization_barrier(jnp.max(jnp.where(visible, scores, -1e+30), axis=-1, keepdims=True))
        expo = jnp.where(visible, jnp.exp(scores - top), 0.0)
        weights = (expo / lax.optimization_barrier(jnp.sum(expo, axis=-1, keepdims=True))).astype(jnp.bfloat16)
        return jnp.einsum('rgnk,rkd->rngd', weights.astype(jnp.float32), kh[:, :, HD:].astype(jnp.float32)).astype(jnp.bfloat16)
    heads_out = lax.map(one_head, (qheads, kheads))
    attended = heads_out.transpose(1, 2, 0, 3, 4).reshape(REQ * NEW, H * HD)
    block = (xf + jnp.dot(attended, wo, preferred_element_type=jnp.float32)).astype(jnp.bfloat16)
    units = fresh.transpose(0, 2, 1, 3).reshape(REQ * KVH, NEW, 2 * HD)
    cache = jnp.zeros((REQ * KVH, NEW, 2 * HD), jnp.bfloat16).at[place].set(units)
    return (block, cache)

def reference(hidden, norm_gain, w_query, w_keyval, w_out, kv_pool, page_table, prefix_len, decode_place):
    rows = REQ * NEW
    blocks = []
    caches = []
    for section in range(N_SECTION):
        block, cache = layer(hidden[section * rows:(section + 1) * rows], norm_gain[section], w_query[section], w_keyval[section], w_out[section], kv_pool[section], page_table[section], prefix_len[section], decode_place[section])
        blocks.append(block)
        caches.append(cache)
    stacked = jnp.stack(blocks, axis=0)
    handed = jnp.roll(stacked, 1, axis=0).reshape(N_SECTION * rows, D)
    return (handed, jnp.stack(caches, axis=0))
```

```python
import functools

import jax
import jax.numpy as jnp
from jax import lax
from jax.experimental import pallas as pl
from jax.experimental.pallas import tpu as pltpu
from jax.sharding import PartitionSpec as P

KVH = 8
HD = 128
PAGE = 128
REQ = 4
NEW = 64


rope_theta = 500000.0


def from_behind(value, axis, steps):
    count = lax.axis_size(axis)
    pairs = [(source, (source + steps) % count) for source in range(count)]
    return lax.ppermute(value, axis, pairs)


def rotate(values, positions, dims, apply, head_size):
    rows = values.shape[0]
    cols = values.shape[1]
    inverse = jnp.power(rope_theta, -(dims // 2 * 2).astype(jnp.float32) / head_size)
    angle = positions[:, None].astype(jnp.float32) * inverse[None, :]
    cosine = jnp.cos(angle)[:, 0::2]
    sine = jnp.sin(angle)[:, 0::2]
    pairs = values.reshape(rows, cols // 2, 2)
    even = pairs[:, :, 0]
    odd = pairs[:, :, 1]
    turned = jnp.stack([even * cosine - odd * sine, even * sine + odd * cosine], axis=-1).reshape(
        rows, cols
    )
    return jnp.where(apply[None, :], turned, values)


def attend(qheads, prefix_kv, fresh_kv, lens):
    prefix = prefix_kv.shape[1]
    count = qheads.shape[1]
    scale = HD ** (-0.5)
    score_pre = (
        jnp.einsum(
            "rnhd,rkd->rhnk", qheads, prefix_kv[:, :, :HD], preferred_element_type=jnp.float32
        )
        * scale
    )
    score_new = (
        jnp.einsum(
            "rnhd,rkd->rhnk", qheads, fresh_kv[:, :, :HD], preferred_element_type=jnp.float32
        )
        * scale
    )
    seen_pre = (jnp.arange(prefix, dtype=jnp.int32)[None, :] < lens[:, None])[:, None, None, :]
    npos = jnp.arange(count, dtype=jnp.int32)
    seen_new = (npos[None, :] <= npos[:, None])[None, None, :, :]
    top = jnp.maximum(
        jnp.max(jnp.where(seen_pre, score_pre, -1e30), axis=-1, keepdims=True),
        jnp.max(jnp.where(seen_new, score_new, -1e30), axis=-1, keepdims=True),
    )
    expo_pre = jnp.where(seen_pre, jnp.exp(score_pre - top), 0.0)
    expo_new = jnp.where(seen_new, jnp.exp(score_new - top), 0.0)
    total = jnp.sum(expo_pre, axis=-1, keepdims=True) + jnp.sum(expo_new, axis=-1, keepdims=True)
    weight_pre = (expo_pre / total).astype(jnp.bfloat16)
    weight_new = (expo_new / total).astype(jnp.bfloat16)
    mixed = jnp.einsum(
        "rhnk,rkd->rnhd", weight_pre, prefix_kv[:, :, HD:], preferred_element_type=jnp.float32
    )
    mixed = mixed + jnp.einsum(
        "rhnk,rkd->rnhd", weight_new, fresh_kv[:, :, HD:], preferred_element_type=jnp.float32
    )
    return mixed.astype(jnp.bfloat16)


def local(
    hidden, norm_gain, w_query, w_keyval, w_out, kv_pool, page_table, prefix_len, decode_place
):
    tp_count = lax.axis_size("tp")
    tp_rank = lax.axis_index("tp")
    w_q = w_query[0]
    w_kv = w_keyval[0]
    w_o = w_out[0]
    q_cols = w_q.shape[1]
    kv_cols = w_kv.shape[1]
    rows_dev = hidden.shape[0]
    xf = hidden.astype(jnp.float32)
    meansq = jnp.mean(xf * xf, axis=-1, keepdims=True)
    normed = (xf * lax.rsqrt(meansq + 1e-05) * norm_gain[0][None, :]).astype(jnp.bfloat16)
    project_piece = lax.all_gather(normed, "tp", axis=0, tiled=True)
    projected = jnp.concatenate(
        [
            jnp.dot(project_piece, w_q, preferred_element_type=jnp.float32),
            jnp.dot(project_piece, w_kv, preferred_element_type=jnp.float32),
        ],
        axis=1,
    )
    lens = prefix_len[0]
    positions = (lens[:, None] + jnp.arange(NEW, dtype=jnp.int32)[None, :]).reshape(-1)
    qdims = jnp.arange(q_cols, dtype=jnp.int32)
    query = rotate(projected[:, :q_cols], positions, qdims % HD, qdims >= 0, HD).astype(
        jnp.bfloat16
    )
    kdims = tp_rank * kv_cols + jnp.arange(kv_cols, dtype=jnp.int32)
    keyval = rotate(projected[:, q_cols:], positions, kdims % HD, kdims // HD % 2 == 0, HD).astype(
        jnp.bfloat16
    )
    keyval_all = lax.all_gather(keyval, "tp", axis=1, tiled=True)
    pool_local = kv_pool[0]
    pool_dev = pool_local.shape[0]
    table_flat = page_table[0]
    listed = table_flat.shape[0] // REQ
    prefix = listed * PAGE
    heads_dev = q_cols // HD
    members = tp_count // KVH
    kv_head = tp_rank // members
    by_head = pool_local.reshape(pool_dev, PAGE, KVH, 2 * HD).transpose(2, 0, 1, 3)
    outgoing = jnp.repeat(by_head, members, axis=0)
    received = lax.all_to_all(outgoing, "tp", split_axis=0, concat_axis=0, tiled=True)
    flat_pages = received.reshape(-1, PAGE, 2 * HD)
    prefix_kv = flat_pages[table_flat.reshape(REQ, listed)].reshape(REQ, prefix, 2 * HD)
    fresh_kv = lax.dynamic_slice_in_dim(keyval_all, kv_head * 2 * HD, 2 * HD, 1).reshape(
        REQ, NEW, 2 * HD
    )
    qheads = query.reshape(REQ, NEW, heads_dev, HD)
    attended = attend(qheads, prefix_kv, fresh_kv, lens).reshape(REQ * NEW, q_cols)
    summed = lax.psum(
        jnp.dot(attended, w_o, preferred_element_type=jnp.float32).astype(jnp.bfloat16), "tp"
    ).astype(jnp.float32)
    mine = lax.dynamic_slice_in_dim(summed, tp_rank * rows_dev, rows_dev, 0)
    block = (xf + mine).astype(jnp.bfloat16)
    handed = from_behind(block, "section", 1)
    slots_dev = REQ * KVH // tp_count
    places = decode_place[0]
    units = keyval_all.reshape(REQ, NEW, KVH, 2 * HD)
    unit_ids = jnp.arange(REQ * KVH, dtype=jnp.int32)
    pieces = []
    for slot in range(slots_dev):
        wanted = tp_rank * slots_dev + slot
        unit = jnp.sum(jnp.where(places == wanted, unit_ids, 0))
        request = unit // KVH
        head = unit % KVH
        zero = jnp.zeros((), jnp.int32)
        piece = lax.dynamic_slice(units, (request, zero, head, zero), (1, NEW, 1, 2 * HD))
        pieces.append(piece.reshape(NEW, 2 * HD))
    decode_cache = jnp.stack(pieces, axis=0)[None]
    return (handed, decode_cache)


MESH = pl.DeviceIdType.MESH
CHUNKS = 4
TILE = 256
HALF = 16


def ring_place(t, n):
    z, y = lax.div(t, 2), lax.rem(t, 2)
    return (1 - y) * z + y * (n - 1 - z)


def ring_member(p, n):
    half = n // 2
    far = lax.div(p, half)
    return (1 - far) * (2 * p) + far * (2 * (n - 1 - p) + 1)


def layer_kernel(
    n,
    n_section,
    hidden_ref,
    gain_ref,
    wq_hbm,
    wkv_hbm,
    wo_hbm,
    pool_hbm,
    cos_ref,
    sin_ref,
    table_ref,
    lens_ref,
    place_ref,
    handed_hbm,
    cache_ref,
    xg,
    wq,
    wkv,
    wo,
    pages,
    acc,
    qs,
    fresh,
    kbuf,
    att,
    rs_half,
    rs_full,
    block,
    w_sem,
    own_sem,
    ag_send,
    ag_recv,
    pg_send,
    pg_recv,
    kv_send,
    kv_recv,
    rs_send,
    rs_recv,
    hand_send,
    hand_recv,
):
    sec = lax.axis_index("section")
    me = lax.axis_index("tp")
    rows, width = hidden_ref.shape
    chunk = width // CHUNKS
    q_cols = wq.shape[1]
    heads = q_cols // HD
    pool_dev = pool_hbm.shape[0]
    listed = table_ref.shape[0] // REQ
    prefix = listed * PAGE
    ring = ring_place(me, n)
    next_sec = lax.rem(sec + 1, n_section)
    prev_sec = lax.rem(sec + n_section - 1, n_section)

    def at_ring(offset):
        return ring_member(lax.rem(ring + offset + 2 * n, n), n)

    barrier = pltpu.get_barrier_semaphore()
    for k in range(1, n):
        pl.semaphore_signal(
            barrier, inc=1, device_id=(sec, lax.rem(me + k, n)), device_id_type=MESH
        )
    for other in (next_sec, prev_sec):
        pl.semaphore_signal(barrier, inc=1, device_id=(other, me), device_id_type=MESH)

    loads = []
    for c in range(CHUNKS):
        part = pl.ds(c * chunk, chunk)
        first = pltpu.make_async_copy(wq_hbm.at[part, :], wq.at[part, :], w_sem.at[3 * c])
        second = pltpu.make_async_copy(wkv_hbm.at[part, :], wkv.at[part, :], w_sem.at[3 * c + 1])
        loads.append((first, second))
        first.start()
        second.start()
    out_loads = []
    for c in range(CHUNKS):
        part = pl.ds(c * chunk, chunk)
        out_loads.append(
            pltpu.make_async_copy(wo_hbm.at[:, part], wo.at[:, part], w_sem.at[3 * c + 2])
        )
        out_loads[-1].start()
    pair = 2 * HD
    own_pages = pltpu.make_async_copy(
        pool_hbm.at[:, :, pl.ds(pl.multiple_of(me * pair, pair), pair)],
        pages.at[pl.ds(me * pool_dev, pool_dev)],
        own_sem,
    )
    own_pages.start()

    xf = hidden_ref[...].astype(jnp.float32)
    meansq = jnp.mean(xf * xf, axis=-1, keepdims=True)
    normed = (xf * lax.rsqrt(meansq + 1e-05) * gain_ref[...]).astype(jnp.bfloat16)
    xg[pl.ds(pl.multiple_of(me * rows, rows), rows), :] = normed

    pl.semaphore_wait(barrier, n - 1 + 2)

    steps = n // 2

    def ag_part(direction, step, c, offset):
        start = at_ring(offset) * rows
        count = rows
        if step == steps:
            start = start + direction * HALF
            count = HALF
        return xg.at[pl.ds(pl.multiple_of(start, count), count), pl.ds(c * chunk, chunk)]

    def ag_copy(direction, step, c):
        sign = 1 - 2 * direction
        index = (direction * steps + step - 1) * CHUNKS + c
        ref = ag_part(direction, step, c, -sign * (step - 1))
        return pltpu.make_async_remote_copy(
            src_ref=ref,
            dst_ref=ref,
            send_sem=ag_send.at[index],
            recv_sem=ag_recv.at[index],
            device_id=(sec, at_ring(sign)),
            device_id_type=MESH,
        )

    def ag_arrived(direction, step, c):
        sign = 1 - 2 * direction
        index = (direction * steps + step - 1) * CHUNKS + c
        ref = ag_part(direction, step, c, -sign * step)
        pltpu.make_async_remote_copy(
            src_ref=ref,
            dst_ref=ref,
            send_sem=ag_send.at[index],
            recv_sem=ag_recv.at[index],
            device_id=(sec, at_ring(sign)),
            device_id_type=MESH,
        ).wait_recv()

    def page_copy(k):
        peer = lax.rem(me + k, n)
        return pltpu.make_async_remote_copy(
            src_ref=pool_hbm.at[:, :, pl.ds(pl.multiple_of(peer * pair, pair), pair)],
            dst_ref=pages.at[pl.ds(me * pool_dev, pool_dev)],
            send_sem=pg_send.at[k],
            recv_sem=pg_recv.at[k],
            device_id=(sec, peer),
            device_id_type=MESH,
        )

    def page_arrived(k):
        peer = lax.rem(me + n - k, n)
        pltpu.make_async_remote_copy(
            src_ref=pool_hbm.at[:, :, pl.ds(pl.multiple_of(me * pair, pair), pair)],
            dst_ref=pages.at[pl.ds(peer * pool_dev, pool_dev)],
            send_sem=pg_send.at[k],
            recv_sem=pg_recv.at[k],
            device_id=(sec, peer),
            device_id_type=MESH,
        ).wait_recv()

    order = sorted(range(1, n), key=lambda k: (abs(k - n // 2), k))
    ag_copies = []
    for c in range(CHUNKS):
        for direction in range(2):
            copy = ag_copy(direction, 1, c)
            copy.start()
            ag_copies.append(copy)
    page_copies = [page_copy(k) for k in order]
    for copy in page_copies:
        copy.start()
    for step in range(2, steps + 1):
        for c in range(CHUNKS):
            for direction in range(2):
                ag_arrived(direction, step - 1, c)
                copy = ag_copy(direction, step, c)
                copy.start()
                ag_copies.append(copy)

    tiles = q_cols // TILE
    for c in range(CHUNKS):
        part = pl.ds(c * chunk, chunk)
        for direction in range(2):
            ag_arrived(direction, steps, c)
        for load in loads[c]:
            load.wait()

        def project(i, carry, c=c, part=part):
            cols = pl.ds(pl.multiple_of(i * TILE, TILE), TILE)
            term = jnp.dot(xg[:, part], wq[part, cols], preferred_element_type=jnp.float32)
            acc[:, cols] = term if c == 0 else acc[:, cols] + term
            return carry

        lax.fori_loop(0, tiles, project, 0)
        term = jnp.dot(xg[:, part], wkv[part, :], preferred_element_type=jnp.float32)
        cols = pl.ds(q_cols, pair)
        acc[:, cols] = term if c == 0 else acc[:, cols] + term

    cosine = cos_ref[...]
    sine = sin_ref[...]
    even = lax.rem(lax.broadcasted_iota(jnp.int32, cosine.shape, 1), 2) == 0

    def turn(values):
        other = jnp.where(even, pltpu.roll(values, HD - 1, 1), pltpu.roll(values, 1, 1))
        return (values * cosine + other * sine).astype(jnp.bfloat16)

    new_rows = REQ * NEW
    key = turn(acc[:, q_cols : q_cols + HD]).reshape(REQ, NEW, HD)
    value = acc[:, q_cols + HD : q_cols + pair].astype(jnp.bfloat16).reshape(REQ, NEW, HD)
    fresh[me, :, :, :HD] = key
    fresh[me, :, :, HD:] = value

    def fresh_copy(k, outgoing):
        peer = lax.rem(me + k, n) if outgoing else lax.rem(me + n - k, n)
        ref = fresh.at[me if outgoing else peer]
        return pltpu.make_async_remote_copy(
            src_ref=ref,
            dst_ref=ref,
            send_sem=kv_send.at[k],
            recv_sem=kv_recv.at[k],
            device_id=(sec, peer),
            device_id_type=MESH,
        )

    fresh_copies = [fresh_copy(k, True) for k in range(1, n)]
    for copy in fresh_copies:
        copy.start()
    for h in range(heads):
        turned = turn(acc[:, h * HD : (h + 1) * HD])
        qs[:, h * NEW : (h + 1) * NEW, :] = turned.reshape(REQ, NEW, HD)

    own_pages.wait()
    for k in order:
        page_arrived(k)

    kbuf[pl.ds(prefix + NEW, NEW), :] = jnp.zeros((NEW, pair), jnp.bfloat16)
    group = heads // 2
    grows = group * NEW
    span = prefix + 2 * NEW
    column = lax.broadcasted_iota(jnp.int32, (grows, span), 1)
    token = lax.rem(lax.broadcasted_iota(jnp.int32, (grows, span), 0), NEW)

    def one_request(r, carry):
        for j in range(listed):
            kbuf[pl.ds(j * PAGE, PAGE), :] = pages[table_ref[r * listed + j]]
        kbuf[pl.ds(prefix, NEW), :] = fresh[me, r]
        limit = jnp.where(column < prefix, lens_ref[r], prefix + 1 + token)
        seen = column < limit
        for part in range(2):
            q = qs[r, part * grows : (part + 1) * grows, :]
            scores = lax.dot_general(
                q, kbuf[:, :HD], (((1,), (1,)), ((), ())), preferred_element_type=jnp.float32
            )
            scores = jnp.where(seen, scores * HD ** (-0.5), -1e30)
            top = jnp.max(scores, axis=-1, keepdims=True)
            expo = jnp.where(seen, jnp.exp(scores - top), 0.0)
            total = jnp.sum(expo, axis=-1, keepdims=True)
            weights = (expo * (1.0 / total)).astype(jnp.bfloat16)
            mixed = jnp.dot(weights, kbuf[:, HD:], preferred_element_type=jnp.float32)
            mixed = mixed.astype(jnp.bfloat16)
            for h in range(group):
                col = (part * group + h) * HD
                att[r, :, col : col + HD] = mixed[h * NEW : (h + 1) * NEW, :]
        return carry

    lax.fori_loop(0, REQ, one_request, 0)

    for copy in ag_copies:
        copy.wait_send()

    def rs_rows(offset):
        return pl.ds(pl.multiple_of(at_ring(offset) * rows, rows), rows)

    def rs_copy(direction, step, c):
        sign = 1 - 2 * direction
        index = (direction * steps + step - 1) * CHUNKS + c
        part = pl.ds(c * chunk, chunk)
        if step == 1:
            start = at_ring(sign * steps) * rows + direction * HALF
            src = xg.at[pl.ds(pl.multiple_of(start, HALF), HALF), part]
            dst = rs_half.at[direction, c]
        else:
            src = xg.at[rs_rows(sign * (steps + 1 - step)), part]
            dst = rs_full.at[direction, step - 2, c]
        return pltpu.make_async_remote_copy(
            src_ref=src,
            dst_ref=dst,
            send_sem=rs_send.at[index],
            recv_sem=rs_recv.at[index],
            device_id=(sec, at_ring(sign)),
            device_id_type=MESH,
        )

    product_tile = min(2 * TILE, chunk)
    rs_copies = {}
    for c in range(CHUNKS):
        out_loads[c].wait()

        def product(i, carry, c=c):
            cols = pl.ds(pl.multiple_of(c * chunk + i * product_tile, product_tile), product_tile)
            xg[:, cols] = jnp.dot(
                att[...].reshape(new_rows, q_cols),
                wo[:, cols],
                preferred_element_type=jnp.float32,
            ).astype(jnp.bfloat16)
            return carry

        lax.fori_loop(0, chunk // product_tile, product, 0)
        for direction in range(2):
            copy = rs_copy(direction, 1, c)
            copy.start()
            rs_copies[direction, 1, c] = copy
    for step in range(2, steps + 1):
        for c in range(CHUNKS):
            part = pl.ds(c * chunk, chunk)
            for direction in range(2):
                sign = 1 - 2 * direction
                rs_copies[direction, step - 1, c].wait_recv()
                if step == 2:
                    start = at_ring(sign * (steps - 1)) * rows + direction * HALF
                    mine = pl.ds(pl.multiple_of(start, HALF), HALF)
                    came = rs_half[direction, c]
                else:
                    mine = rs_rows(sign * (steps + 1 - step))
                    came = rs_full[direction, step - 3, c]
                xg[mine, part] = (
                    xg[mine, part].astype(jnp.float32) + came.astype(jnp.float32)
                ).astype(jnp.bfloat16)
                copy = rs_copy(direction, step, c)
                copy.start()
                rs_copies[direction, step, c] = copy

    hands = []
    own = pl.ds(pl.multiple_of(me * rows, rows), rows)
    for c in range(CHUNKS):
        part = pl.ds(c * chunk, chunk)
        for direction in range(2):
            rs_copies[direction, steps, c].wait_recv()
        summed = xg[own, part].astype(jnp.float32)
        for direction in range(2):
            summed = summed + rs_full[direction, steps - 2, c].astype(jnp.float32)
        block[:, part] = (hidden_ref[:, part].astype(jnp.float32) + summed).astype(jnp.bfloat16)
        hand = pltpu.make_async_remote_copy(
            src_ref=block.at[:, part],
            dst_ref=handed_hbm.at[:, part],
            send_sem=hand_send.at[c],
            recv_sem=hand_recv.at[c],
            device_id=(next_sec, me),
            device_id_type=MESH,
        )
        hand.start()
        hands.append(hand)

    for k in range(1, n):
        fresh_copy(k, False).wait_recv()
    slots = cache_ref.shape[0]
    units = place_ref.shape[0]
    for slot in range(slots):
        wanted = me * slots + slot
        unit = jnp.int32(0)
        for u in range(units):
            unit = jnp.where(place_ref[u] == wanted, u, unit)
        cache_ref[slot] = fresh[lax.rem(unit, KVH), lax.div(unit, KVH)]

    for copy in page_copies:
        copy.wait_send()
    for copy in fresh_copies:
        copy.wait_send()
    for copy in rs_copies.values():
        copy.wait_send()
    for hand in hands:
        hand.wait()


def fused(
    n,
    n_section,
    hidden,
    norm_gain,
    w_query,
    w_keyval,
    w_out,
    kv_pool,
    page_table,
    prefix_len,
    decode_place,
):
    rows, width = hidden.shape
    q_cols = w_query.shape[2]
    pool_dev = kv_pool.shape[1]
    pair = 2 * HD
    new_rows = REQ * NEW
    prefix = page_table.shape[1] // REQ * PAGE
    slots = REQ * KVH // n
    steps = n // 2
    chunk = width // CHUNKS
    heads = q_cols // HD
    lens = prefix_len[0]
    positions = (lens[:, None] + jnp.arange(NEW, dtype=jnp.int32)[None, :]).reshape(-1)
    dims = jnp.arange(HD, dtype=jnp.int32)
    inverse = jnp.power(rope_theta, -(dims // 2 * 2).astype(jnp.float32) / HD)
    angle = positions[:, None].astype(jnp.float32) * inverse[None, :]
    cosine = jnp.cos(angle)
    sine = jnp.where(dims[None, :] % 2 == 0, -jnp.sin(angle), jnp.sin(angle))
    vmem = pl.BlockSpec(memory_space=pltpu.VMEM)
    smem = pl.BlockSpec(memory_space=pltpu.SMEM)
    far = pl.BlockSpec(memory_space=pl.ANY)
    bf16 = jnp.bfloat16
    dma = pltpu.SemaphoreType.DMA
    handed, cache = pl.pallas_call(
        functools.partial(layer_kernel, n, n_section),
        out_shape=(
            jax.ShapeDtypeStruct((rows, width), bf16),
            jax.ShapeDtypeStruct((slots, NEW, pair), bf16),
        ),
        in_specs=[vmem, vmem, far, far, far, far, vmem, vmem, smem, smem, smem],
        out_specs=(far, vmem),
        scratch_shapes=[
            pltpu.VMEM((new_rows, width), bf16),
            pltpu.VMEM((width, q_cols), bf16),
            pltpu.VMEM((width, pair), bf16),
            pltpu.VMEM((q_cols, width), bf16),
            pltpu.VMEM((n * pool_dev, PAGE, pair), bf16),
            pltpu.VMEM((new_rows, q_cols + pair), jnp.float32),
            pltpu.VMEM((REQ, heads * NEW, HD), bf16),
            pltpu.VMEM((n, REQ, NEW, pair), bf16),
            pltpu.VMEM((prefix + 2 * NEW, pair), bf16),
            pltpu.VMEM((REQ, NEW, q_cols), bf16),
            pltpu.VMEM((2, CHUNKS, HALF, chunk), bf16),
            pltpu.VMEM((2, steps - 1, CHUNKS, rows, chunk), bf16),
            pltpu.VMEM((rows, width), bf16),
            dma((3 * CHUNKS,)),
            dma,
            dma((2 * steps * CHUNKS,)),
            dma((2 * steps * CHUNKS,)),
            dma((n,)),
            dma((n,)),
            dma((n,)),
            dma((n,)),
            dma((2 * steps * CHUNKS,)),
            dma((2 * steps * CHUNKS,)),
            dma((CHUNKS,)),
            dma((CHUNKS,)),
        ],
        compiler_params=pltpu.CompilerParams(
            collective_id=0, has_side_effects=True, vmem_limit_bytes=60 * 1024 * 1024
        ),
        cost_estimate=pl.CostEstimate(
            flops=11_000_000_000, bytes_accessed=40_000_000, transcendentals=2_000_000
        ),
    )(
        hidden,
        norm_gain,
        w_query[0],
        w_keyval[0],
        w_out[0],
        kv_pool[0],
        cosine,
        sine,
        page_table[0],
        lens,
        decode_place[0],
    )
    return (handed, cache[None])


def solution(mesh):
    placed = (
        P(("section", "tp"), None),
        P("section", None),
        P("section", None, "tp"),
        P("section", None, "tp"),
        P("section", "tp", None),
        P("section", "tp", None, None),
        P("section", None),
        P("section", None),
        P("section", None),
    )
    n = mesh.shape["tp"]
    body = local
    if n == KVH:
        body = functools.partial(fused, n, mesh.shape["section"])
    return jax.shard_map(
        body,
        mesh=mesh,
        in_specs=placed,
        out_specs=(P(("section", "tp"), None), P("section", "tp", None, None)),
        check_vma=False,
    )
```

```python
import functools

import jax
import jax.numpy as jnp
from jax import lax
from jax.experimental import pallas as pl
from jax.experimental.pallas import tpu as pltpu
from jax.sharding import PartitionSpec as P

KVH = 8
HD = 128
PAGE = 128
REQ = 4
NEW = 64


rope_theta = 500000.0


def from_behind(value, axis, steps):
    count = lax.axis_size(axis)
    pairs = [(source, (source + steps) % count) for source in range(count)]
    return lax.ppermute(value, axis, pairs)


def rotate(values, positions, dims, apply, head_size):
    rows = values.shape[0]
    cols = values.shape[1]
    inverse = jnp.power(rope_theta, -(dims // 2 * 2).astype(jnp.float32) / head_size)
    angle = positions[:, None].astype(jnp.float32) * inverse[None, :]
    cosine = jnp.cos(angle)[:, 0::2]
    sine = jnp.sin(angle)[:, 0::2]
    pairs = values.reshape(rows, cols // 2, 2)
    even = pairs[:, :, 0]
    odd = pairs[:, :, 1]
    turned = jnp.stack([even * cosine - odd * sine, even * sine + odd * cosine], axis=-1).reshape(
        rows, cols
    )
    return jnp.where(apply[None, :], turned, values)


def attend(qheads, prefix_kv, fresh_kv, lens):
    prefix = prefix_kv.shape[1]
    count = qheads.shape[1]
    scale = HD ** (-0.5)
    score_pre = (
        jnp.einsum(
            "rnhd,rkd->rhnk", qheads, prefix_kv[:, :, :HD], preferred_element_type=jnp.float32
        )
        * scale
    )
    score_new = (
        jnp.einsum(
            "rnhd,rkd->rhnk", qheads, fresh_kv[:, :, :HD], preferred_element_type=jnp.float32
        )
        * scale
    )
    seen_pre = (jnp.arange(prefix, dtype=jnp.int32)[None, :] < lens[:, None])[:, None, None, :]
    npos = jnp.arange(count, dtype=jnp.int32)
    seen_new = (npos[None, :] <= npos[:, None])[None, None, :, :]
    top = jnp.maximum(
        jnp.max(jnp.where(seen_pre, score_pre, -1e30), axis=-1, keepdims=True),
        jnp.max(jnp.where(seen_new, score_new, -1e30), axis=-1, keepdims=True),
    )
    expo_pre = jnp.where(seen_pre, jnp.exp(score_pre - top), 0.0)
    expo_new = jnp.where(seen_new, jnp.exp(score_new - top), 0.0)
    total = jnp.sum(expo_pre, axis=-1, keepdims=True) + jnp.sum(expo_new, axis=-1, keepdims=True)
    weight_pre = (expo_pre / total).astype(jnp.bfloat16)
    weight_new = (expo_new / total).astype(jnp.bfloat16)
    mixed = jnp.einsum(
        "rhnk,rkd->rnhd", weight_pre, prefix_kv[:, :, HD:], preferred_element_type=jnp.float32
    )
    mixed = mixed + jnp.einsum(
        "rhnk,rkd->rnhd", weight_new, fresh_kv[:, :, HD:], preferred_element_type=jnp.float32
    )
    return mixed.astype(jnp.bfloat16)


def local(
    hidden, norm_gain, w_query, w_keyval, w_out, kv_pool, page_table, prefix_len, decode_place
):
    tp_count = lax.axis_size("tp")
    tp_rank = lax.axis_index("tp")
    w_q = w_query[0]
    w_kv = w_keyval[0]
    w_o = w_out[0]
    q_cols = w_q.shape[1]
    kv_cols = w_kv.shape[1]
    rows_dev = hidden.shape[0]
    xf = hidden.astype(jnp.float32)
    meansq = jnp.mean(xf * xf, axis=-1, keepdims=True)
    normed = (xf * lax.rsqrt(meansq + 1e-05) * norm_gain[0][None, :]).astype(jnp.bfloat16)
    project_piece = lax.all_gather(normed, "tp", axis=0, tiled=True)
    projected = jnp.concatenate(
        [
            jnp.dot(project_piece, w_q, preferred_element_type=jnp.float32),
            jnp.dot(project_piece, w_kv, preferred_element_type=jnp.float32),
        ],
        axis=1,
    )
    lens = prefix_len[0]
    positions = (lens[:, None] + jnp.arange(NEW, dtype=jnp.int32)[None, :]).reshape(-1)
    qdims = jnp.arange(q_cols, dtype=jnp.int32)
    query = rotate(projected[:, :q_cols], positions, qdims % HD, qdims >= 0, HD).astype(
        jnp.bfloat16
    )
    kdims = tp_rank * kv_cols + jnp.arange(kv_cols, dtype=jnp.int32)
    keyval = rotate(projected[:, q_cols:], positions, kdims % HD, kdims // HD % 2 == 0, HD).astype(
        jnp.bfloat16
    )
    keyval_all = lax.all_gather(keyval, "tp", axis=1, tiled=True)
    pool_local = kv_pool[0]
    pool_dev = pool_local.shape[0]
    table_flat = page_table[0]
    listed = table_flat.shape[0] // REQ
    prefix = listed * PAGE
    heads_dev = q_cols // HD
    members = tp_count // KVH
    kv_head = tp_rank // members
    by_head = pool_local.reshape(pool_dev, PAGE, KVH, 2 * HD).transpose(2, 0, 1, 3)
    outgoing = jnp.repeat(by_head, members, axis=0)
    received = lax.all_to_all(outgoing, "tp", split_axis=0, concat_axis=0, tiled=True)
    flat_pages = received.reshape(-1, PAGE, 2 * HD)
    prefix_kv = flat_pages[table_flat.reshape(REQ, listed)].reshape(REQ, prefix, 2 * HD)
    fresh_kv = lax.dynamic_slice_in_dim(keyval_all, kv_head * 2 * HD, 2 * HD, 1).reshape(
        REQ, NEW, 2 * HD
    )
    qheads = query.reshape(REQ, NEW, heads_dev, HD)
    attended = attend(qheads, prefix_kv, fresh_kv, lens).reshape(REQ * NEW, q_cols)
    summed = lax.psum(
        jnp.dot(attended, w_o, preferred_element_type=jnp.float32).astype(jnp.bfloat16), "tp"
    ).astype(jnp.float32)
    mine = lax.dynamic_slice_in_dim(summed, tp_rank * rows_dev, rows_dev, 0)
    block = (xf + mine).astype(jnp.bfloat16)
    handed = from_behind(block, "section", 1)
    slots_dev = REQ * KVH // tp_count
    places = decode_place[0]
    units = keyval_all.reshape(REQ, NEW, KVH, 2 * HD)
    unit_ids = jnp.arange(REQ * KVH, dtype=jnp.int32)
    pieces = []
    for slot in range(slots_dev):
        wanted = tp_rank * slots_dev + slot
        unit = jnp.sum(jnp.where(places == wanted, unit_ids, 0))
        request = unit // KVH
        head = unit % KVH
        zero = jnp.zeros((), jnp.int32)
        piece = lax.dynamic_slice(units, (request, zero, head, zero), (1, NEW, 1, 2 * HD))
        pieces.append(piece.reshape(NEW, 2 * HD))
    decode_cache = jnp.stack(pieces, axis=0)[None]
    return (handed, decode_cache)


MESH = pl.DeviceIdType.MESH
CHUNKS = 4
TILE = 256
HALF = 16


def ring_place(t, n):
    z, y = lax.div(t, 2), lax.rem(t, 2)
    return (1 - y) * z + y * (n - 1 - z)


def ring_member(p, n):
    half = n // 2
    far = lax.div(p, half)
    return (1 - far) * (2 * p) + far * (2 * (n - 1 - p) + 1)


def layer_kernel(
    n,
    n_section,
    hidden_ref,
    gain_ref,
    wq_hbm,
    wkv_hbm,
    wo_hbm,
    pool_hbm,
    inverse_ref,
    table_ref,
    lens_ref,
    place_ref,
    handed_hbm,
    cache_ref,
    xg,
    wq,
    wkv,
    wo,
    pages,
    acc,
    qs,
    fresh,
    kbuf,
    att,
    rs_half,
    rs_full,
    block,
    cosine,
    sine,
    w_sem,
    own_sem,
    ag_send,
    ag_recv,
    pg_send,
    pg_recv,
    kv_send,
    kv_recv,
    rs_send,
    rs_recv,
    hand_send,
    hand_recv,
):
    sec = lax.axis_index("section")
    me = lax.axis_index("tp")
    rows, width = hidden_ref.shape
    chunk = width // CHUNKS
    q_cols = wq.shape[1]
    heads = q_cols // HD
    pool_dev = pool_hbm.shape[0]
    listed = table_ref.shape[0] // REQ
    prefix = listed * PAGE
    ring = ring_place(me, n)
    next_sec = lax.rem(sec + 1, n_section)
    prev_sec = lax.rem(sec + n_section - 1, n_section)

    def at_ring(offset):
        return ring_member(lax.rem(ring + offset + 2 * n, n), n)

    barrier = pltpu.get_barrier_semaphore()
    for k in range(1, n):
        pl.semaphore_signal(
            barrier, inc=1, device_id=(sec, lax.rem(me + k, n)), device_id_type=MESH
        )
    for other in (next_sec, prev_sec):
        pl.semaphore_signal(barrier, inc=1, device_id=(other, me), device_id_type=MESH)

    loads = []
    for c in range(CHUNKS):
        part = pl.ds(c * chunk, chunk)
        first = pltpu.make_async_copy(wq_hbm.at[part, :], wq.at[part, :], w_sem.at[3 * c])
        second = pltpu.make_async_copy(wkv_hbm.at[part, :], wkv.at[part, :], w_sem.at[3 * c + 1])
        loads.append((first, second))
        first.start()
        second.start()
    out_loads = []
    for c in range(CHUNKS):
        part = pl.ds(c * chunk, chunk)
        out_loads.append(
            pltpu.make_async_copy(wo_hbm.at[:, part], wo.at[:, part], w_sem.at[3 * c + 2])
        )
        out_loads[-1].start()
    pair = 2 * HD
    own_pages = pltpu.make_async_copy(
        pool_hbm.at[:, :, pl.ds(pl.multiple_of(me * pair, pair), pair)],
        pages.at[pl.ds(me * pool_dev, pool_dev)],
        own_sem,
    )
    own_pages.start()

    xf = hidden_ref[...].astype(jnp.float32)
    meansq = jnp.mean(xf * xf, axis=-1, keepdims=True)
    normed = (xf * lax.rsqrt(meansq + 1e-05) * gain_ref[...]).astype(jnp.bfloat16)
    xg[pl.ds(pl.multiple_of(me * rows, rows), rows), :] = normed

    pl.semaphore_wait(barrier, n - 1 + 2)

    steps = n // 2
    line = n // 2
    z, y = lax.div(me, 2), lax.rem(me, 2)

    def ag_copy(kind, step, c, outgoing):
        sign = 1 - 2 * (kind % 2)
        if kind < 2:
            far = z - sign * (step - 1 if outgoing else step)
            side = y
            peer = lax.rem(z + sign + line, line) * 2 + y
        else:
            far = z - sign * step
            side = y if outgoing else 1 - y
            peer = z * 2 + 1 - y
        start = (lax.rem(far + line, line) * 2 + side) * rows
        ref = xg.at[pl.ds(pl.multiple_of(start, rows), rows), pl.ds(c * chunk, chunk)]
        index = (kind * line + step) * CHUNKS + c
        return pltpu.make_async_remote_copy(
            src_ref=ref,
            dst_ref=ref,
            send_sem=ag_send.at[index],
            recv_sem=ag_recv.at[index],
            device_id=(sec, peer),
            device_id_type=MESH,
        )

    def holds(kind, step):
        return z >= step if kind % 2 == 0 else z <= line - 1 - step

    def goes_on(kind):
        return z <= line - 2 if kind % 2 == 0 else z >= 1

    def page_copy(k):
        peer = lax.rem(me + k, n)
        return pltpu.make_async_remote_copy(
            src_ref=pool_hbm.at[:, :, pl.ds(pl.multiple_of(peer * pair, pair), pair)],
            dst_ref=pages.at[pl.ds(me * pool_dev, pool_dev)],
            send_sem=pg_send.at[k],
            recv_sem=pg_recv.at[k],
            device_id=(sec, peer),
            device_id_type=MESH,
        )

    def page_arrived(k):
        peer = lax.rem(me + n - k, n)
        pltpu.make_async_remote_copy(
            src_ref=pool_hbm.at[:, :, pl.ds(pl.multiple_of(me * pair, pair), pair)],
            dst_ref=pages.at[pl.ds(peer * pool_dev, pool_dev)],
            send_sem=pg_send.at[k],
            recv_sem=pg_recv.at[k],
            device_id=(sec, peer),
            device_id_type=MESH,
        ).wait_recv()

    order = sorted(range(1, n), key=lambda k: (abs(k - n // 2), k))
    for c in range(CHUNKS):
        for kind in range(2):

            @pl.when(goes_on(kind))
            def _(kind=kind, c=c):
                ag_copy(kind, 1, c, True).start()

        ag_copy(2, 0, c, True).start()
    page_copies = [page_copy(k) for k in order]
    for copy in page_copies:
        copy.start()

    row_ids = lax.broadcasted_iota(jnp.int32, cosine.shape, 0)
    request = lax.div(row_ids, NEW)
    position = lax.rem(row_ids, NEW)
    for r in range(REQ):
        position = position + jnp.where(request == r, lens_ref[r], 0)
    even = lax.rem(lax.broadcasted_iota(jnp.int32, cosine.shape, 1), 2) == 0
    angle = position.astype(jnp.float32) * inverse_ref[...]
    cosine[...] = jnp.cos(angle)
    turned_sine = jnp.sin(angle)
    sine[...] = jnp.where(even, -turned_sine, turned_sine)

    for step in range(1, line):
        for c in range(CHUNKS):
            for kind in range(2):

                @pl.when(holds(kind, step))
                def _(kind=kind, step=step, c=c):
                    ag_copy(kind, step, c, False).wait_recv()
                    if step < line - 1:

                        @pl.when(goes_on(kind))
                        def _():
                            ag_copy(kind, step + 1, c, True).start()

                    ag_copy(kind + 2, step, c, True).start()

    tiles = q_cols // TILE
    for c in range(CHUNKS):
        part = pl.ds(c * chunk, chunk)
        ag_copy(2, 0, c, False).wait_recv()
        for step in range(1, line):
            for kind in range(2, 4):

                @pl.when(holds(kind, step))
                def _(kind=kind, step=step, c=c):
                    ag_copy(kind, step, c, False).wait_recv()

        for load in loads[c]:
            load.wait()

        def project(i, carry, c=c, part=part):
            cols = pl.ds(pl.multiple_of(i * TILE, TILE), TILE)
            term = jnp.dot(xg[:, part], wq[part, cols], preferred_element_type=jnp.float32)
            acc[:, cols] = term if c == 0 else acc[:, cols] + term
            return carry

        lax.fori_loop(0, tiles, project, 0)
        term = jnp.dot(xg[:, part], wkv[part, :], preferred_element_type=jnp.float32)
        cols = pl.ds(q_cols, pair)
        acc[:, cols] = term if c == 0 else acc[:, cols] + term

    def turn(values):
        other = jnp.where(even, pltpu.roll(values, HD - 1, 1), pltpu.roll(values, 1, 1))
        return (values * cosine[...] + other * sine[...]).astype(jnp.bfloat16)

    new_rows = REQ * NEW
    key = turn(acc[:, q_cols : q_cols + HD]).reshape(REQ, NEW, HD)
    value = acc[:, q_cols + HD : q_cols + pair].astype(jnp.bfloat16).reshape(REQ, NEW, HD)
    fresh[me, :, :, :HD] = key
    fresh[me, :, :, HD:] = value

    def fresh_copy(k, outgoing):
        peer = lax.rem(me + k, n) if outgoing else lax.rem(me + n - k, n)
        ref = fresh.at[me if outgoing else peer]
        return pltpu.make_async_remote_copy(
            src_ref=ref,
            dst_ref=ref,
            send_sem=kv_send.at[k],
            recv_sem=kv_recv.at[k],
            device_id=(sec, peer),
            device_id_type=MESH,
        )

    fresh_copies = [fresh_copy(k, True) for k in range(1, n)]
    for copy in fresh_copies:
        copy.start()
    for h in range(heads):
        turned = turn(acc[:, h * HD : (h + 1) * HD])
        qs[:, h * NEW : (h + 1) * NEW, :] = turned.reshape(REQ, NEW, HD)

    own_pages.wait()
    for k in order:
        page_arrived(k)

    kbuf[pl.ds(prefix + NEW, NEW), :] = jnp.zeros((NEW, pair), jnp.bfloat16)
    group = heads // 2
    grows = group * NEW
    span = prefix + 2 * NEW
    column = lax.broadcasted_iota(jnp.int32, (grows, span), 1)
    token = lax.rem(lax.broadcasted_iota(jnp.int32, (grows, span), 0), NEW)

    def one_request(r, carry):
        for j in range(listed):
            kbuf[pl.ds(j * PAGE, PAGE), :] = pages[table_ref[r * listed + j]]
        kbuf[pl.ds(prefix, NEW), :] = fresh[me, r]
        limit = jnp.where(column < prefix, lens_ref[r], prefix + 1 + token)
        seen = column < limit
        for part in range(2):
            q = qs[r, part * grows : (part + 1) * grows, :]
            scores = lax.dot_general(
                q, kbuf[:, :HD], (((1,), (1,)), ((), ())), preferred_element_type=jnp.float32
            )
            scores = jnp.where(seen, scores * HD ** (-0.5), -1e30)
            top = jnp.max(scores, axis=-1, keepdims=True)
            expo = jnp.where(seen, jnp.exp(scores - top), 0.0)
            total = jnp.sum(expo, axis=-1, keepdims=True)
            weights = (expo * (1.0 / total)).astype(jnp.bfloat16)
            mixed = jnp.dot(weights, kbuf[:, HD:], preferred_element_type=jnp.float32)
            mixed = mixed.astype(jnp.bfloat16)
            for h in range(group):
                col = (part * group + h) * HD
                att[r, :, col : col + HD] = mixed[h * NEW : (h + 1) * NEW, :]
        return carry

    lax.fori_loop(0, REQ, one_request, 0)

    for c in range(CHUNKS):
        ag_copy(2, 0, c, True).wait_send()
        for step in range(1, line):
            for kind in range(2):

                @pl.when(holds(kind, step - 1) & goes_on(kind))
                def _(kind=kind, step=step, c=c):
                    ag_copy(kind, step, c, True).wait_send()

                @pl.when(holds(kind, step))
                def _(kind=kind, step=step, c=c):
                    ag_copy(kind + 2, step, c, True).wait_send()

    def rs_rows(offset):
        return pl.ds(pl.multiple_of(at_ring(offset) * rows, rows), rows)

    def rs_copy(direction, step, c):
        sign = 1 - 2 * direction
        index = (direction * steps + step - 1) * CHUNKS + c
        part = pl.ds(c * chunk, chunk)
        if step == 1:
            start = at_ring(sign * steps) * rows + direction * HALF
            src = xg.at[pl.ds(pl.multiple_of(start, HALF), HALF), part]
            dst = rs_half.at[direction, c]
        else:
            src = xg.at[rs_rows(sign * (steps + 1 - step)), part]
            dst = rs_full.at[direction, step - 2, c]
        return pltpu.make_async_remote_copy(
            src_ref=src,
            dst_ref=dst,
            send_sem=rs_send.at[index],
            recv_sem=rs_recv.at[index],
            device_id=(sec, at_ring(sign)),
            device_id_type=MESH,
        )

    product_tile = min(2 * TILE, chunk)
    rs_copies = {}
    for c in range(CHUNKS):
        out_loads[c].wait()

        def product(i, carry, c=c):
            cols = pl.ds(pl.multiple_of(c * chunk + i * product_tile, product_tile), product_tile)
            xg[:, cols] = jnp.dot(
                att[...].reshape(new_rows, q_cols),
                wo[:, cols],
                preferred_element_type=jnp.float32,
            ).astype(jnp.bfloat16)
            return carry

        lax.fori_loop(0, chunk // product_tile, product, 0)
        for direction in range(2):
            copy = rs_copy(direction, 1, c)
            copy.start()
            rs_copies[direction, 1, c] = copy
    for step in range(2, steps + 1):
        for c in range(CHUNKS):
            part = pl.ds(c * chunk, chunk)
            for direction in range(2):
                sign = 1 - 2 * direction
                rs_copies[direction, step - 1, c].wait_recv()
                if step == 2:
                    start = at_ring(sign * (steps - 1)) * rows + direction * HALF
                    mine = pl.ds(pl.multiple_of(start, HALF), HALF)
                    came = rs_half[direction, c]
                else:
                    mine = rs_rows(sign * (steps + 1 - step))
                    came = rs_full[direction, step - 3, c]
                xg[mine, part] = (
                    xg[mine, part].astype(jnp.float32) + came.astype(jnp.float32)
                ).astype(jnp.bfloat16)
                copy = rs_copy(direction, step, c)
                copy.start()
                rs_copies[direction, step, c] = copy

    hands = []
    own = pl.ds(pl.multiple_of(me * rows, rows), rows)
    for c in range(CHUNKS):
        part = pl.ds(c * chunk, chunk)
        for direction in range(2):
            rs_copies[direction, steps, c].wait_recv()
        summed = xg[own, part].astype(jnp.float32)
        for direction in range(2):
            summed = summed + rs_full[direction, steps - 2, c].astype(jnp.float32)
        block[:, part] = (hidden_ref[:, part].astype(jnp.float32) + summed).astype(jnp.bfloat16)
        hand = pltpu.make_async_remote_copy(
            src_ref=block.at[:, part],
            dst_ref=handed_hbm.at[:, part],
            send_sem=hand_send.at[c],
            recv_sem=hand_recv.at[c],
            device_id=(next_sec, me),
            device_id_type=MESH,
        )
        hand.start()
        hands.append(hand)

    for k in range(1, n):
        fresh_copy(k, False).wait_recv()
    slots = cache_ref.shape[0]
    units = place_ref.shape[0]
    for slot in range(slots):
        wanted = me * slots + slot
        unit = jnp.int32(0)
        for u in range(units):
            unit = jnp.where(place_ref[u] == wanted, u, unit)
        cache_ref[slot] = fresh[lax.rem(unit, KVH), lax.div(unit, KVH)]

    for copy in page_copies:
        copy.wait_send()
    for copy in fresh_copies:
        copy.wait_send()
    for copy in rs_copies.values():
        copy.wait_send()
    for hand in hands:
        hand.wait()


def fused(
    n,
    n_section,
    hidden,
    norm_gain,
    w_query,
    w_keyval,
    w_out,
    kv_pool,
    page_table,
    prefix_len,
    decode_place,
):
    rows, width = hidden.shape
    q_cols = w_query.shape[2]
    pool_dev = kv_pool.shape[1]
    pair = 2 * HD
    new_rows = REQ * NEW
    prefix = page_table.shape[1] // REQ * PAGE
    slots = REQ * KVH // n
    steps = n // 2
    chunk = width // CHUNKS
    heads = q_cols // HD
    lens = prefix_len[0]
    dims = jnp.arange(HD, dtype=jnp.int32)
    inverse = jnp.power(rope_theta, -(dims // 2 * 2).astype(jnp.float32) / HD)[None, :]
    vmem = pl.BlockSpec(memory_space=pltpu.VMEM)
    smem = pl.BlockSpec(memory_space=pltpu.SMEM)
    far = pl.BlockSpec(memory_space=pl.ANY)
    bf16 = jnp.bfloat16
    dma = pltpu.SemaphoreType.DMA
    handed, cache = pl.pallas_call(
        functools.partial(layer_kernel, n, n_section),
        out_shape=(
            jax.ShapeDtypeStruct((rows, width), bf16),
            jax.ShapeDtypeStruct((slots, NEW, pair), bf16),
        ),
        in_specs=[vmem, vmem, far, far, far, far, vmem, smem, smem, smem],
        out_specs=(far, vmem),
        scratch_shapes=[
            pltpu.VMEM((new_rows, width), bf16),
            pltpu.VMEM((width, q_cols), bf16),
            pltpu.VMEM((width, pair), bf16),
            pltpu.VMEM((q_cols, width), bf16),
            pltpu.VMEM((n * pool_dev, PAGE, pair), bf16),
            pltpu.VMEM((new_rows, q_cols + pair), jnp.float32),
            pltpu.VMEM((REQ, heads * NEW, HD), bf16),
            pltpu.VMEM((n, REQ, NEW, pair), bf16),
            pltpu.VMEM((prefix + 2 * NEW, pair), bf16),
            pltpu.VMEM((REQ, NEW, q_cols), bf16),
            pltpu.VMEM((2, CHUNKS, HALF, chunk), bf16),
            pltpu.VMEM((2, steps - 1, CHUNKS, rows, chunk), bf16),
            pltpu.VMEM((rows, width), bf16),
            pltpu.VMEM((new_rows, HD), jnp.float32),
            pltpu.VMEM((new_rows, HD), jnp.float32),
            dma((3 * CHUNKS,)),
            dma,
            dma((4 * steps * CHUNKS,)),
            dma((4 * steps * CHUNKS,)),
            dma((n,)),
            dma((n,)),
            dma((n,)),
            dma((n,)),
            dma((2 * steps * CHUNKS,)),
            dma((2 * steps * CHUNKS,)),
            dma((CHUNKS,)),
            dma((CHUNKS,)),
        ],
        compiler_params=pltpu.CompilerParams(
            collective_id=0, has_side_effects=True, vmem_limit_bytes=60 * 1024 * 1024
        ),
        cost_estimate=pl.CostEstimate(
            flops=11_000_000_000, bytes_accessed=40_000_000, transcendentals=2_000_000
        ),
    )(
        hidden,
        norm_gain,
        w_query[0],
        w_keyval[0],
        w_out[0],
        kv_pool[0],
        inverse,
        page_table[0],
        lens,
        decode_place[0],
    )
    return (handed, cache[None])


def solution(mesh):
    placed = (
        P(("section", "tp"), None),
        P("section", None),
        P("section", None, "tp"),
        P("section", None, "tp"),
        P("section", "tp", None),
        P("section", "tp", None, None),
        P("section", None),
        P("section", None),
        P("section", None),
    )
    n = mesh.shape["tp"]
    body = local
    if n == KVH:
        body = functools.partial(fused, n, mesh.shape["section"])
    return jax.shard_map(
        body,
        mesh=mesh,
        in_specs=placed,
        out_specs=(P(("section", "tp"), None), P("section", "tp", None, None)),
        check_vma=False,
    )
```

```python
import functools

import jax
import jax.numpy as jnp
from jax import lax
from jax.experimental import pallas as pl
from jax.experimental.pallas import tpu as pltpu
from jax.sharding import PartitionSpec as P

KVH = 8
HD = 128
PAGE = 128
REQ = 4
NEW = 64


rope_theta = 500000.0


def from_behind(value, axis, steps):
    count = lax.axis_size(axis)
    pairs = [(source, (source + steps) % count) for source in range(count)]
    return lax.ppermute(value, axis, pairs)


def rotate(values, positions, dims, apply, head_size):
    rows = values.shape[0]
    cols = values.shape[1]
    inverse = jnp.power(rope_theta, -(dims // 2 * 2).astype(jnp.float32) / head_size)
    angle = positions[:, None].astype(jnp.float32) * inverse[None, :]
    cosine = jnp.cos(angle)[:, 0::2]
    sine = jnp.sin(angle)[:, 0::2]
    pairs = values.reshape(rows, cols // 2, 2)
    even = pairs[:, :, 0]
    odd = pairs[:, :, 1]
    turned = jnp.stack([even * cosine - odd * sine, even * sine + odd * cosine], axis=-1).reshape(
        rows, cols
    )
    return jnp.where(apply[None, :], turned, values)


def attend(qheads, prefix_kv, fresh_kv, lens):
    prefix = prefix_kv.shape[1]
    count = qheads.shape[1]
    scale = HD ** (-0.5)
    score_pre = (
        jnp.einsum(
            "rnhd,rkd->rhnk", qheads, prefix_kv[:, :, :HD], preferred_element_type=jnp.float32
        )
        * scale
    )
    score_new = (
        jnp.einsum(
            "rnhd,rkd->rhnk", qheads, fresh_kv[:, :, :HD], preferred_element_type=jnp.float32
        )
        * scale
    )
    seen_pre = (jnp.arange(prefix, dtype=jnp.int32)[None, :] < lens[:, None])[:, None, None, :]
    npos = jnp.arange(count, dtype=jnp.int32)
    seen_new = (npos[None, :] <= npos[:, None])[None, None, :, :]
    top = jnp.maximum(
        jnp.max(jnp.where(seen_pre, score_pre, -1e30), axis=-1, keepdims=True),
        jnp.max(jnp.where(seen_new, score_new, -1e30), axis=-1, keepdims=True),
    )
    expo_pre = jnp.where(seen_pre, jnp.exp(score_pre - top), 0.0)
    expo_new = jnp.where(seen_new, jnp.exp(score_new - top), 0.0)
    total = jnp.sum(expo_pre, axis=-1, keepdims=True) + jnp.sum(expo_new, axis=-1, keepdims=True)
    weight_pre = (expo_pre / total).astype(jnp.bfloat16)
    weight_new = (expo_new / total).astype(jnp.bfloat16)
    mixed = jnp.einsum(
        "rhnk,rkd->rnhd", weight_pre, prefix_kv[:, :, HD:], preferred_element_type=jnp.float32
    )
    mixed = mixed + jnp.einsum(
        "rhnk,rkd->rnhd", weight_new, fresh_kv[:, :, HD:], preferred_element_type=jnp.float32
    )
    return mixed.astype(jnp.bfloat16)


def local(
    hidden, norm_gain, w_query, w_keyval, w_out, kv_pool, page_table, prefix_len, decode_place
):
    tp_count = lax.axis_size("tp")
    tp_rank = lax.axis_index("tp")
    w_q = w_query[0]
    w_kv = w_keyval[0]
    w_o = w_out[0]
    q_cols = w_q.shape[1]
    kv_cols = w_kv.shape[1]
    rows_dev = hidden.shape[0]
    xf = hidden.astype(jnp.float32)
    meansq = jnp.mean(xf * xf, axis=-1, keepdims=True)
    normed = (xf * lax.rsqrt(meansq + 1e-05) * norm_gain[0][None, :]).astype(jnp.bfloat16)
    project_piece = lax.all_gather(normed, "tp", axis=0, tiled=True)
    projected = jnp.concatenate(
        [
            jnp.dot(project_piece, w_q, preferred_element_type=jnp.float32),
            jnp.dot(project_piece, w_kv, preferred_element_type=jnp.float32),
        ],
        axis=1,
    )
    lens = prefix_len[0]
    positions = (lens[:, None] + jnp.arange(NEW, dtype=jnp.int32)[None, :]).reshape(-1)
    qdims = jnp.arange(q_cols, dtype=jnp.int32)
    query = rotate(projected[:, :q_cols], positions, qdims % HD, qdims >= 0, HD).astype(
        jnp.bfloat16
    )
    kdims = tp_rank * kv_cols + jnp.arange(kv_cols, dtype=jnp.int32)
    keyval = rotate(projected[:, q_cols:], positions, kdims % HD, kdims // HD % 2 == 0, HD).astype(
        jnp.bfloat16
    )
    keyval_all = lax.all_gather(keyval, "tp", axis=1, tiled=True)
    pool_local = kv_pool[0]
    pool_dev = pool_local.shape[0]
    table_flat = page_table[0]
    listed = table_flat.shape[0] // REQ
    prefix = listed * PAGE
    heads_dev = q_cols // HD
    members = tp_count // KVH
    kv_head = tp_rank // members
    by_head = pool_local.reshape(pool_dev, PAGE, KVH, 2 * HD).transpose(2, 0, 1, 3)
    outgoing = jnp.repeat(by_head, members, axis=0)
    received = lax.all_to_all(outgoing, "tp", split_axis=0, concat_axis=0, tiled=True)
    flat_pages = received.reshape(-1, PAGE, 2 * HD)
    prefix_kv = flat_pages[table_flat.reshape(REQ, listed)].reshape(REQ, prefix, 2 * HD)
    fresh_kv = lax.dynamic_slice_in_dim(keyval_all, kv_head * 2 * HD, 2 * HD, 1).reshape(
        REQ, NEW, 2 * HD
    )
    qheads = query.reshape(REQ, NEW, heads_dev, HD)
    attended = attend(qheads, prefix_kv, fresh_kv, lens).reshape(REQ * NEW, q_cols)
    summed = lax.psum(
        jnp.dot(attended, w_o, preferred_element_type=jnp.float32).astype(jnp.bfloat16), "tp"
    ).astype(jnp.float32)
    mine = lax.dynamic_slice_in_dim(summed, tp_rank * rows_dev, rows_dev, 0)
    block = (xf + mine).astype(jnp.bfloat16)
    handed = from_behind(block, "section", 1)
    slots_dev = REQ * KVH // tp_count
    places = decode_place[0]
    units = keyval_all.reshape(REQ, NEW, KVH, 2 * HD)
    unit_ids = jnp.arange(REQ * KVH, dtype=jnp.int32)
    pieces = []
    for slot in range(slots_dev):
        wanted = tp_rank * slots_dev + slot
        unit = jnp.sum(jnp.where(places == wanted, unit_ids, 0))
        request = unit // KVH
        head = unit % KVH
        zero = jnp.zeros((), jnp.int32)
        piece = lax.dynamic_slice(units, (request, zero, head, zero), (1, NEW, 1, 2 * HD))
        pieces.append(piece.reshape(NEW, 2 * HD))
    decode_cache = jnp.stack(pieces, axis=0)[None]
    return (handed, decode_cache)


MESH = pl.DeviceIdType.MESH
CHUNKS = 4
TILE = 256
HALF = 16


def ring_place(t, n):
    z, y = lax.div(t, 2), lax.rem(t, 2)
    return (1 - y) * z + y * (n - 1 - z)


def ring_member(p, n):
    half = n // 2
    far = lax.div(p, half)
    return (1 - far) * (2 * p) + far * (2 * (n - 1 - p) + 1)


def layer_kernel(
    n,
    n_section,
    hidden_ref,
    gain_ref,
    wq_hbm,
    wkv_hbm,
    wo_hbm,
    pool_hbm,
    inverse_ref,
    table_ref,
    lens_ref,
    place_ref,
    handed_hbm,
    cache_ref,
    xg,
    wq,
    wkv,
    wo,
    pages,
    acc,
    qs,
    fresh,
    kbuf,
    att,
    rs_half,
    rs_full,
    block,
    cosine,
    sine,
    w_sem,
    own_sem,
    ag_send,
    ag_recv,
    pg_send,
    pg_recv,
    kv_send,
    kv_recv,
    rs_send,
    rs_recv,
    hand_send,
    hand_recv,
):
    sec = lax.axis_index("section")
    me = lax.axis_index("tp")
    rows, width = hidden_ref.shape
    chunk = width // CHUNKS
    q_cols = wq.shape[1]
    heads = q_cols // HD
    pool_dev = pool_hbm.shape[0]
    listed = table_ref.shape[0] // REQ
    prefix = listed * PAGE
    ring = ring_place(me, n)
    next_sec = lax.rem(sec + 1, n_section)
    prev_sec = lax.rem(sec + n_section - 1, n_section)

    def at_ring(offset):
        return ring_member(lax.rem(ring + offset + 2 * n, n), n)

    barrier = pltpu.get_barrier_semaphore()
    for k in range(1, n):
        pl.semaphore_signal(
            barrier, inc=1, device_id=(sec, lax.rem(me + k, n)), device_id_type=MESH
        )
    for other in (next_sec, prev_sec):
        pl.semaphore_signal(barrier, inc=1, device_id=(other, me), device_id_type=MESH)

    loads = []
    for c in range(CHUNKS):
        part = pl.ds(c * chunk, chunk)
        first = pltpu.make_async_copy(wq_hbm.at[part, :], wq.at[part, :], w_sem.at[3 * c])
        second = pltpu.make_async_copy(wkv_hbm.at[part, :], wkv.at[part, :], w_sem.at[3 * c + 1])
        loads.append((first, second))
        first.start()
        second.start()
    out_loads = []
    for c in range(CHUNKS):
        part = pl.ds(c * chunk, chunk)
        out_loads.append(
            pltpu.make_async_copy(wo_hbm.at[:, part], wo.at[:, part], w_sem.at[3 * c + 2])
        )
        out_loads[-1].start()
    pair = 2 * HD
    own_pages = pltpu.make_async_copy(
        pool_hbm.at[:, :, pl.ds(pl.multiple_of(me * pair, pair), pair)],
        pages.at[pl.ds(me * pool_dev, pool_dev)],
        own_sem,
    )
    own_pages.start()

    xf = hidden_ref[...].astype(jnp.float32)
    meansq = jnp.mean(xf * xf, axis=-1, keepdims=True)
    normed = (xf * lax.rsqrt(meansq + 1e-05) * gain_ref[...]).astype(jnp.bfloat16)
    xg[pl.ds(pl.multiple_of(me * rows, rows), rows), :] = normed

    pl.semaphore_wait(barrier, n - 1 + 2)

    steps = n // 2
    line = n // 2
    z, y = lax.div(me, 2), lax.rem(me, 2)

    def ag_copy(kind, step, c, outgoing):
        sign = 1 - 2 * (kind % 2)
        if kind < 2:
            far = z - sign * (step - 1 if outgoing else step)
            side = y
            peer = lax.rem(z + sign + line, line) * 2 + y
        else:
            far = z - sign * step
            side = y if outgoing else 1 - y
            peer = z * 2 + 1 - y
        start = (lax.rem(far + line, line) * 2 + side) * rows
        ref = xg.at[pl.ds(pl.multiple_of(start, rows), rows), pl.ds(c * chunk, chunk)]
        index = (kind * line + step) * CHUNKS + c
        return pltpu.make_async_remote_copy(
            src_ref=ref,
            dst_ref=ref,
            send_sem=ag_send.at[index],
            recv_sem=ag_recv.at[index],
            device_id=(sec, peer),
            device_id_type=MESH,
        )

    def holds(kind, step):
        return z >= step if kind % 2 == 0 else z <= line - 1 - step

    def goes_on(kind):
        return z <= line - 2 if kind % 2 == 0 else z >= 1

    def page_copy(k):
        peer = lax.rem(me + k, n)
        return pltpu.make_async_remote_copy(
            src_ref=pool_hbm.at[:, :, pl.ds(pl.multiple_of(peer * pair, pair), pair)],
            dst_ref=pages.at[pl.ds(me * pool_dev, pool_dev)],
            send_sem=pg_send.at[k],
            recv_sem=pg_recv.at[k],
            device_id=(sec, peer),
            device_id_type=MESH,
        )

    def page_arrived(k):
        peer = lax.rem(me + n - k, n)
        pltpu.make_async_remote_copy(
            src_ref=pool_hbm.at[:, :, pl.ds(pl.multiple_of(me * pair, pair), pair)],
            dst_ref=pages.at[pl.ds(peer * pool_dev, pool_dev)],
            send_sem=pg_send.at[k],
            recv_sem=pg_recv.at[k],
            device_id=(sec, peer),
            device_id_type=MESH,
        ).wait_recv()

    order = sorted(range(1, n), key=lambda k: (k % 2, abs(k - n // 2), k))
    slots_ahead = [0, 1, 3, 6, 7, 9, 10]
    for c in range(CHUNKS):
        for kind in range(2):

            @pl.when(goes_on(kind))
            def _(kind=kind, c=c):
                ag_copy(kind, 1, c, True).start()

        ag_copy(2, 0, c, True).start()
    page_copies = [page_copy(k) for k in order]
    page_copies[0].start()
    started = 1

    row_ids = lax.broadcasted_iota(jnp.int32, cosine.shape, 0)
    request = lax.div(row_ids, NEW)
    position = lax.rem(row_ids, NEW)
    for r in range(REQ):
        position = position + jnp.where(request == r, lens_ref[r], 0)
    even = lax.rem(lax.broadcasted_iota(jnp.int32, cosine.shape, 1), 2) == 0
    angle = position.astype(jnp.float32) * inverse_ref[...]
    cosine[...] = jnp.cos(angle)
    turned_sine = jnp.sin(angle)
    sine[...] = jnp.where(even, -turned_sine, turned_sine)

    for step in range(1, line):
        for c in range(CHUNKS):
            for kind in range(2):

                @pl.when(holds(kind, step))
                def _(kind=kind, step=step, c=c):
                    ag_copy(kind, step, c, False).wait_recv()
                    if step < line - 1:

                        @pl.when(goes_on(kind))
                        def _():
                            ag_copy(kind, step + 1, c, True).start()

                    ag_copy(kind + 2, step, c, True).start()

            slot = (step - 1) * CHUNKS + c + 1
            while started < n - 1 and slots_ahead[started] <= slot:
                page_copies[started].start()
                started += 1
    tiles = q_cols // TILE
    for c in range(CHUNKS):
        part = pl.ds(c * chunk, chunk)
        ag_copy(2, 0, c, False).wait_recv()
        for step in range(1, line):
            for kind in range(2, 4):

                @pl.when(holds(kind, step))
                def _(kind=kind, step=step, c=c):
                    ag_copy(kind, step, c, False).wait_recv()

        for load in loads[c]:
            load.wait()

        def project(i, carry, c=c, part=part):
            cols = pl.ds(pl.multiple_of(i * TILE, TILE), TILE)
            term = jnp.dot(xg[:, part], wq[part, cols], preferred_element_type=jnp.float32)
            acc[:, cols] = term if c == 0 else acc[:, cols] + term
            return carry

        lax.fori_loop(0, tiles, project, 0)
        term = jnp.dot(xg[:, part], wkv[part, :], preferred_element_type=jnp.float32)
        cols = pl.ds(q_cols, pair)
        acc[:, cols] = term if c == 0 else acc[:, cols] + term

    def turn(values):
        other = jnp.where(even, pltpu.roll(values, HD - 1, 1), pltpu.roll(values, 1, 1))
        return (values * cosine[...] + other * sine[...]).astype(jnp.bfloat16)

    new_rows = REQ * NEW
    key = turn(acc[:, q_cols : q_cols + HD]).reshape(REQ, NEW, HD)
    value = acc[:, q_cols + HD : q_cols + pair].astype(jnp.bfloat16).reshape(REQ, NEW, HD)
    fresh[me, :, :, :HD] = key
    fresh[me, :, :, HD:] = value

    def fresh_copy(k, outgoing):
        peer = lax.rem(me + k, n) if outgoing else lax.rem(me + n - k, n)
        ref = fresh.at[me if outgoing else peer]
        return pltpu.make_async_remote_copy(
            src_ref=ref,
            dst_ref=ref,
            send_sem=kv_send.at[k],
            recv_sem=kv_recv.at[k],
            device_id=(sec, peer),
            device_id_type=MESH,
        )

    fresh_copies = [fresh_copy(k, True) for k in range(1, n)]
    for copy in fresh_copies:
        copy.start()
    for h in range(heads):
        turned = turn(acc[:, h * HD : (h + 1) * HD])
        qs[:, h * NEW : (h + 1) * NEW, :] = turned.reshape(REQ, NEW, HD)

    own_pages.wait()
    for k in order:
        page_arrived(k)

    kbuf[pl.ds(prefix + NEW, NEW), :] = jnp.zeros((NEW, pair), jnp.bfloat16)
    group = heads // 2
    grows = group * NEW
    prefix_column = lax.broadcasted_iota(jnp.int32, (grows, prefix), 1)
    fresh_column = lax.broadcasted_iota(jnp.int32, (grows, 2 * NEW), 1)
    token = lax.rem(lax.broadcasted_iota(jnp.int32, (grows, 2 * NEW), 0), NEW)
    causal = fresh_column <= token
    factor = HD ** (-0.5) * 1.4426950408889634
    contract = (((1,), (1,)), ((), ()))

    def one_request(r, carry):
        for j in range(listed):
            kbuf[pl.ds(j * PAGE, PAGE), :] = pages[table_ref[r * listed + j]]
        kbuf[pl.ds(prefix, NEW), :] = fresh[me, r]
        limit = lens_ref[r]
        for part in range(2):
            q = qs[r, part * grows : (part + 1) * grows, :]
            old = lax.dot_general(
                q, kbuf[:prefix, :HD], contract, preferred_element_type=jnp.float32
            )
            new = lax.dot_general(
                q, kbuf[prefix:, :HD], contract, preferred_element_type=jnp.float32
            )
            old = jnp.where(prefix_column < limit, old, -1e30)
            new = jnp.where(causal, new, -1e30)
            top = jnp.maximum(
                jnp.max(old, axis=-1, keepdims=True), jnp.max(new, axis=-1, keepdims=True)
            )
            old = jnp.exp2((old - top) * factor)
            new = jnp.exp2((new - top) * factor)
            total = jnp.sum(old, axis=-1, keepdims=True) + jnp.sum(new, axis=-1, keepdims=True)
            scale = 1.0 / total
            mixed = jnp.dot(
                (old * scale).astype(jnp.bfloat16),
                kbuf[:prefix, HD:],
                preferred_element_type=jnp.float32,
            )
            mixed = mixed + jnp.dot(
                (new * scale).astype(jnp.bfloat16),
                kbuf[prefix:, HD:],
                preferred_element_type=jnp.float32,
            )
            mixed = mixed.astype(jnp.bfloat16)
            for h in range(group):
                col = (part * group + h) * HD
                att[r, :, col : col + HD] = mixed[h * NEW : (h + 1) * NEW, :]
        return carry

    lax.fori_loop(0, REQ, one_request, 0)

    for c in range(CHUNKS):
        ag_copy(2, 0, c, True).wait_send()
        for step in range(1, line):
            for kind in range(2):

                @pl.when(holds(kind, step - 1) & goes_on(kind))
                def _(kind=kind, step=step, c=c):
                    ag_copy(kind, step, c, True).wait_send()

                @pl.when(holds(kind, step))
                def _(kind=kind, step=step, c=c):
                    ag_copy(kind + 2, step, c, True).wait_send()

    def rs_rows(offset):
        return pl.ds(pl.multiple_of(at_ring(offset) * rows, rows), rows)

    def rs_copy(direction, step, c):
        sign = 1 - 2 * direction
        index = (direction * steps + step - 1) * CHUNKS + c
        part = pl.ds(c * chunk, chunk)
        if step == 1:
            start = at_ring(sign * steps) * rows + direction * HALF
            src = xg.at[pl.ds(pl.multiple_of(start, HALF), HALF), part]
            dst = rs_half.at[direction, c]
        else:
            src = xg.at[rs_rows(sign * (steps + 1 - step)), part]
            dst = rs_full.at[direction, step - 2, c]
        return pltpu.make_async_remote_copy(
            src_ref=src,
            dst_ref=dst,
            send_sem=rs_send.at[index],
            recv_sem=rs_recv.at[index],
            device_id=(sec, at_ring(sign)),
            device_id_type=MESH,
        )

    product_tile = min(2 * TILE, chunk)
    rs_copies = {}
    for c in range(CHUNKS):
        out_loads[c].wait()

        def product(i, carry, c=c):
            cols = pl.ds(pl.multiple_of(c * chunk + i * product_tile, product_tile), product_tile)
            xg[:, cols] = jnp.dot(
                att[...].reshape(new_rows, q_cols),
                wo[:, cols],
                preferred_element_type=jnp.float32,
            ).astype(jnp.bfloat16)
            return carry

        lax.fori_loop(0, chunk // product_tile, product, 0)
        for direction in range(2):
            copy = rs_copy(direction, 1, c)
            copy.start()
            rs_copies[direction, 1, c] = copy
    for step in range(2, steps + 1):
        for c in range(CHUNKS):
            part = pl.ds(c * chunk, chunk)
            for direction in range(2):
                sign = 1 - 2 * direction
                rs_copies[direction, step - 1, c].wait_recv()
                if step == 2:
                    start = at_ring(sign * (steps - 1)) * rows + direction * HALF
                    mine = pl.ds(pl.multiple_of(start, HALF), HALF)
                    came = rs_half[direction, c]
                else:
                    mine = rs_rows(sign * (steps + 1 - step))
                    came = rs_full[direction, step - 3, c]
                xg[mine, part] = (
                    xg[mine, part].astype(jnp.float32) + came.astype(jnp.float32)
                ).astype(jnp.bfloat16)
                copy = rs_copy(direction, step, c)
                copy.start()
                rs_copies[direction, step, c] = copy

    hands = []
    own = pl.ds(pl.multiple_of(me * rows, rows), rows)
    for c in range(CHUNKS):
        part = pl.ds(c * chunk, chunk)
        for direction in range(2):
            rs_copies[direction, steps, c].wait_recv()
        summed = xg[own, part].astype(jnp.float32)
        for direction in range(2):
            summed = summed + rs_full[direction, steps - 2, c].astype(jnp.float32)
        block[:, part] = (hidden_ref[:, part].astype(jnp.float32) + summed).astype(jnp.bfloat16)
        hand = pltpu.make_async_remote_copy(
            src_ref=block.at[:, part],
            dst_ref=handed_hbm.at[:, part],
            send_sem=hand_send.at[c],
            recv_sem=hand_recv.at[c],
            device_id=(next_sec, me),
            device_id_type=MESH,
        )
        hand.start()
        hands.append(hand)

    for k in range(1, n):
        fresh_copy(k, False).wait_recv()
    slots = cache_ref.shape[0]
    units = place_ref.shape[0]
    for slot in range(slots):
        wanted = me * slots + slot
        unit = jnp.int32(0)
        for u in range(units):
            unit = jnp.where(place_ref[u] == wanted, u, unit)
        cache_ref[slot] = fresh[lax.rem(unit, KVH), lax.div(unit, KVH)]

    for copy in page_copies:
        copy.wait_send()
    for copy in fresh_copies:
        copy.wait_send()
    for copy in rs_copies.values():
        copy.wait_send()
    for hand in hands:
        hand.wait()


def settle_kernel(handed_in, cache_in, handed_out, cache_out, sems):
    first = pltpu.make_async_copy(handed_in, handed_out, sems.at[0])
    second = pltpu.make_async_copy(cache_in, cache_out, sems.at[1])
    first.start()
    second.start()
    first.wait()
    second.wait()


def fused(
    n,
    n_section,
    hidden,
    norm_gain,
    w_query,
    w_keyval,
    w_out,
    kv_pool,
    page_table,
    prefix_len,
    decode_place,
):
    rows, width = hidden.shape
    q_cols = w_query.shape[2]
    pool_dev = kv_pool.shape[1]
    pair = 2 * HD
    new_rows = REQ * NEW
    prefix = page_table.shape[1] // REQ * PAGE
    slots = REQ * KVH // n
    steps = n // 2
    chunk = width // CHUNKS
    heads = q_cols // HD
    lens = prefix_len[0]
    dims = jnp.arange(HD, dtype=jnp.int32)
    inverse = jnp.power(rope_theta, -(dims // 2 * 2).astype(jnp.float32) / HD)[None, :]
    vmem = pl.BlockSpec(memory_space=pltpu.VMEM)
    smem = pl.BlockSpec(memory_space=pltpu.SMEM)
    far = pl.BlockSpec(memory_space=pl.ANY)
    bf16 = jnp.bfloat16
    dma = pltpu.SemaphoreType.DMA
    handed, cache = pl.pallas_call(
        functools.partial(layer_kernel, n, n_section),
        out_shape=(
            jax.ShapeDtypeStruct((rows, width), bf16),
            jax.ShapeDtypeStruct((slots, NEW, pair), bf16),
        ),
        in_specs=[vmem, vmem, far, far, far, far, vmem, smem, smem, smem],
        out_specs=(far, vmem),
        scratch_shapes=[
            pltpu.VMEM((new_rows, width), bf16),
            pltpu.VMEM((width, q_cols), bf16),
            pltpu.VMEM((width, pair), bf16),
            pltpu.VMEM((q_cols, width), bf16),
            pltpu.VMEM((n * pool_dev, PAGE, pair), bf16),
            pltpu.VMEM((new_rows, q_cols + pair), jnp.float32),
            pltpu.VMEM((REQ, heads * NEW, HD), bf16),
            pltpu.VMEM((n, REQ, NEW, pair), bf16),
            pltpu.VMEM((prefix + 2 * NEW, pair), bf16),
            pltpu.VMEM((REQ, NEW, q_cols), bf16),
            pltpu.VMEM((2, CHUNKS, HALF, chunk), bf16),
            pltpu.VMEM((2, steps - 1, CHUNKS, rows, chunk), bf16),
            pltpu.VMEM((rows, width), bf16),
            pltpu.VMEM((new_rows, HD), jnp.float32),
            pltpu.VMEM((new_rows, HD), jnp.float32),
            dma((3 * CHUNKS,)),
            dma,
            dma((4 * steps * CHUNKS,)),
            dma((4 * steps * CHUNKS,)),
            dma((n,)),
            dma((n,)),
            dma((n,)),
            dma((n,)),
            dma((2 * steps * CHUNKS,)),
            dma((2 * steps * CHUNKS,)),
            dma((CHUNKS,)),
            dma((CHUNKS,)),
        ],
        compiler_params=pltpu.CompilerParams(
            collective_id=0, has_side_effects=True, vmem_limit_bytes=60 * 1024 * 1024
        ),
        cost_estimate=pl.CostEstimate(
            flops=11_000_000_000, bytes_accessed=40_000_000, transcendentals=2_000_000
        ),
    )(
        hidden,
        norm_gain,
        w_query[0],
        w_keyval[0],
        w_out[0],
        kv_pool[0],
        inverse,
        page_table[0],
        lens,
        decode_place[0],
    )
    handed, cache = pl.pallas_call(
        settle_kernel,
        out_shape=(
            jax.ShapeDtypeStruct(handed.shape, bf16),
            jax.ShapeDtypeStruct(cache.shape, bf16),
        ),
        in_specs=[far, far],
        out_specs=(far, far),
        scratch_shapes=[dma((2,))],
        compiler_params=pltpu.CompilerParams(vmem_limit_bytes=60 * 1024 * 1024),
        cost_estimate=pl.CostEstimate(flops=0, bytes_accessed=1_300_000, transcendentals=0),
    )(handed, cache)
    return (handed, cache[None])


def solution(mesh):
    placed = (
        P(("section", "tp"), None),
        P("section", None),
        P("section", None, "tp"),
        P("section", None, "tp"),
        P("section", "tp", None),
        P("section", "tp", None, None),
        P("section", None),
        P("section", None),
        P("section", None),
    )
    n = mesh.shape["tp"]
    body = local
    if n == KVH:
        body = functools.partial(fused, n, mesh.shape["section"])
    return jax.shard_map(
        body,
        mesh=mesh,
        in_specs=placed,
        out_specs=(P(("section", "tp"), None), P("section", "tp", None, None)),
        check_vma=False,
    )
```

```python
import functools

import jax
import jax.numpy as jnp
from jax import lax
from jax.experimental import pallas as pl
from jax.experimental.pallas import tpu as pltpu
from jax.sharding import PartitionSpec as P

KVH = 8
HD = 128
PAGE = 128
REQ = 4
NEW = 64


rope_theta = 500000.0


def from_behind(value, axis, steps):
    count = lax.axis_size(axis)
    pairs = [(source, (source + steps) % count) for source in range(count)]
    return lax.ppermute(value, axis, pairs)


def rotate(values, positions, dims, apply, head_size):
    rows = values.shape[0]
    cols = values.shape[1]
    inverse = jnp.power(rope_theta, -(dims // 2 * 2).astype(jnp.float32) / head_size)
    angle = positions[:, None].astype(jnp.float32) * inverse[None, :]
    cosine = jnp.cos(angle)[:, 0::2]
    sine = jnp.sin(angle)[:, 0::2]
    pairs = values.reshape(rows, cols // 2, 2)
    even = pairs[:, :, 0]
    odd = pairs[:, :, 1]
    turned = jnp.stack([even * cosine - odd * sine, even * sine + odd * cosine], axis=-1).reshape(
        rows, cols
    )
    return jnp.where(apply[None, :], turned, values)


def attend(qheads, prefix_kv, fresh_kv, lens):
    prefix = prefix_kv.shape[1]
    count = qheads.shape[1]
    scale = HD ** (-0.5)
    score_pre = (
        jnp.einsum(
            "rnhd,rkd->rhnk", qheads, prefix_kv[:, :, :HD], preferred_element_type=jnp.float32
        )
        * scale
    )
    score_new = (
        jnp.einsum(
            "rnhd,rkd->rhnk", qheads, fresh_kv[:, :, :HD], preferred_element_type=jnp.float32
        )
        * scale
    )
    seen_pre = (jnp.arange(prefix, dtype=jnp.int32)[None, :] < lens[:, None])[:, None, None, :]
    npos = jnp.arange(count, dtype=jnp.int32)
    seen_new = (npos[None, :] <= npos[:, None])[None, None, :, :]
    top = jnp.maximum(
        jnp.max(jnp.where(seen_pre, score_pre, -1e30), axis=-1, keepdims=True),
        jnp.max(jnp.where(seen_new, score_new, -1e30), axis=-1, keepdims=True),
    )
    expo_pre = jnp.where(seen_pre, jnp.exp(score_pre - top), 0.0)
    expo_new = jnp.where(seen_new, jnp.exp(score_new - top), 0.0)
    total = jnp.sum(expo_pre, axis=-1, keepdims=True) + jnp.sum(expo_new, axis=-1, keepdims=True)
    weight_pre = (expo_pre / total).astype(jnp.bfloat16)
    weight_new = (expo_new / total).astype(jnp.bfloat16)
    mixed = jnp.einsum(
        "rhnk,rkd->rnhd", weight_pre, prefix_kv[:, :, HD:], preferred_element_type=jnp.float32
    )
    mixed = mixed + jnp.einsum(
        "rhnk,rkd->rnhd", weight_new, fresh_kv[:, :, HD:], preferred_element_type=jnp.float32
    )
    return mixed.astype(jnp.bfloat16)


def local(
    hidden, norm_gain, w_query, w_keyval, w_out, kv_pool, page_table, prefix_len, decode_place
):
    tp_count = lax.axis_size("tp")
    tp_rank = lax.axis_index("tp")
    w_q = w_query[0]
    w_kv = w_keyval[0]
    w_o = w_out[0]
    q_cols = w_q.shape[1]
    kv_cols = w_kv.shape[1]
    rows_dev = hidden.shape[0]
    xf = hidden.astype(jnp.float32)
    meansq = jnp.mean(xf * xf, axis=-1, keepdims=True)
    normed = (xf * lax.rsqrt(meansq + 1e-05) * norm_gain[0][None, :]).astype(jnp.bfloat16)
    project_piece = lax.all_gather(normed, "tp", axis=0, tiled=True)
    projected = jnp.concatenate(
        [
            jnp.dot(project_piece, w_q, preferred_element_type=jnp.float32),
            jnp.dot(project_piece, w_kv, preferred_element_type=jnp.float32),
        ],
        axis=1,
    )
    lens = prefix_len[0]
    positions = (lens[:, None] + jnp.arange(NEW, dtype=jnp.int32)[None, :]).reshape(-1)
    qdims = jnp.arange(q_cols, dtype=jnp.int32)
    query = rotate(projected[:, :q_cols], positions, qdims % HD, qdims >= 0, HD).astype(
        jnp.bfloat16
    )
    kdims = tp_rank * kv_cols + jnp.arange(kv_cols, dtype=jnp.int32)
    keyval = rotate(projected[:, q_cols:], positions, kdims % HD, kdims // HD % 2 == 0, HD).astype(
        jnp.bfloat16
    )
    keyval_all = lax.all_gather(keyval, "tp", axis=1, tiled=True)
    pool_local = kv_pool[0]
    pool_dev = pool_local.shape[0]
    table_flat = page_table[0]
    listed = table_flat.shape[0] // REQ
    prefix = listed * PAGE
    heads_dev = q_cols // HD
    members = tp_count // KVH
    kv_head = tp_rank // members
    by_head = pool_local.reshape(pool_dev, PAGE, KVH, 2 * HD).transpose(2, 0, 1, 3)
    outgoing = jnp.repeat(by_head, members, axis=0)
    received = lax.all_to_all(outgoing, "tp", split_axis=0, concat_axis=0, tiled=True)
    flat_pages = received.reshape(-1, PAGE, 2 * HD)
    prefix_kv = flat_pages[table_flat.reshape(REQ, listed)].reshape(REQ, prefix, 2 * HD)
    fresh_kv = lax.dynamic_slice_in_dim(keyval_all, kv_head * 2 * HD, 2 * HD, 1).reshape(
        REQ, NEW, 2 * HD
    )
    qheads = query.reshape(REQ, NEW, heads_dev, HD)
    attended = attend(qheads, prefix_kv, fresh_kv, lens).reshape(REQ * NEW, q_cols)
    summed = lax.psum(
        jnp.dot(attended, w_o, preferred_element_type=jnp.float32).astype(jnp.bfloat16), "tp"
    ).astype(jnp.float32)
    mine = lax.dynamic_slice_in_dim(summed, tp_rank * rows_dev, rows_dev, 0)
    block = (xf + mine).astype(jnp.bfloat16)
    handed = from_behind(block, "section", 1)
    slots_dev = REQ * KVH // tp_count
    places = decode_place[0]
    units = keyval_all.reshape(REQ, NEW, KVH, 2 * HD)
    unit_ids = jnp.arange(REQ * KVH, dtype=jnp.int32)
    pieces = []
    for slot in range(slots_dev):
        wanted = tp_rank * slots_dev + slot
        unit = jnp.sum(jnp.where(places == wanted, unit_ids, 0))
        request = unit // KVH
        head = unit % KVH
        zero = jnp.zeros((), jnp.int32)
        piece = lax.dynamic_slice(units, (request, zero, head, zero), (1, NEW, 1, 2 * HD))
        pieces.append(piece.reshape(NEW, 2 * HD))
    decode_cache = jnp.stack(pieces, axis=0)[None]
    return (handed, decode_cache)


MESH = pl.DeviceIdType.MESH
CHUNKS = 4
TILE = 256
HALF = 16


def ring_place(t, n):
    z, y = lax.div(t, 2), lax.rem(t, 2)
    return (1 - y) * z + y * (n - 1 - z)


def ring_member(p, n):
    half = n // 2
    far = lax.div(p, half)
    return (1 - far) * (2 * p) + far * (2 * (n - 1 - p) + 1)


def layer_kernel(
    n,
    n_section,
    hidden_ref,
    gain_ref,
    wq_hbm,
    wkv_hbm,
    wo_hbm,
    pool_hbm,
    inverse_ref,
    table_ref,
    lens_ref,
    place_ref,
    handed_ref,
    cache_ref,
    xg,
    wq,
    wkv,
    wo,
    pages,
    acc,
    qs,
    fresh,
    kbuf,
    att,
    rs_half,
    rs_full,
    block,
    cosine,
    sine,
    staged,
    w_sem,
    own_sem,
    stage_sem,
    ag_send,
    ag_recv,
    pg_send,
    pg_recv,
    kv_send,
    kv_recv,
    rs_send,
    rs_recv,
    hand_send,
    hand_recv,
):
    sec = lax.axis_index("section")
    me = lax.axis_index("tp")
    rows, width = hidden_ref.shape
    chunk = width // CHUNKS
    q_cols = wq.shape[1]
    heads = q_cols // HD
    pool_dev = pool_hbm.shape[0]
    listed = table_ref.shape[0] // REQ
    prefix = listed * PAGE
    ring = ring_place(me, n)
    next_sec = lax.rem(sec + 1, n_section)
    prev_sec = lax.rem(sec + n_section - 1, n_section)

    def at_ring(offset):
        return ring_member(lax.rem(ring + offset + 2 * n, n), n)

    barrier = pltpu.get_barrier_semaphore()
    for k in range(1, n):
        pl.semaphore_signal(
            barrier, inc=1, device_id=(sec, lax.rem(me + k, n)), device_id_type=MESH
        )
    for other in (next_sec, prev_sec):
        pl.semaphore_signal(barrier, inc=1, device_id=(other, me), device_id_type=MESH)

    pair = 2 * HD

    def page_load(k):
        peer = lax.rem(me + k, n)
        return pltpu.make_async_copy(
            pool_hbm.at[:, :, pl.ds(pl.multiple_of(peer * pair, pair), pair)],
            staged.at[k],
            stage_sem.at[k],
        )

    for k in range(1, n):
        page_load(k).start()
    loads = []
    for c in range(CHUNKS):
        part = pl.ds(c * chunk, chunk)
        first = pltpu.make_async_copy(wq_hbm.at[part, :], wq.at[part, :], w_sem.at[3 * c])
        second = pltpu.make_async_copy(wkv_hbm.at[part, :], wkv.at[part, :], w_sem.at[3 * c + 1])
        loads.append((first, second))
        first.start()
        second.start()
    out_loads = []
    for c in range(CHUNKS):
        part = pl.ds(c * chunk, chunk)
        out_loads.append(
            pltpu.make_async_copy(wo_hbm.at[:, part], wo.at[:, part], w_sem.at[3 * c + 2])
        )
        out_loads[-1].start()
    own_pages = pltpu.make_async_copy(
        pool_hbm.at[:, :, pl.ds(pl.multiple_of(me * pair, pair), pair)],
        pages.at[pl.ds(me * pool_dev, pool_dev)],
        own_sem,
    )
    own_pages.start()

    xf = hidden_ref[...].astype(jnp.float32)
    meansq = jnp.mean(xf * xf, axis=-1, keepdims=True)
    normed = (xf * lax.rsqrt(meansq + 1e-05) * gain_ref[...]).astype(jnp.bfloat16)
    xg[pl.ds(pl.multiple_of(me * rows, rows), rows), :] = normed

    pl.semaphore_wait(barrier, n - 1 + 2)

    steps = n // 2
    line = n // 2
    z, y = lax.div(me, 2), lax.rem(me, 2)

    def ag_copy(kind, step, c, outgoing):
        sign = 1 - 2 * (kind % 2)
        if kind < 2:
            far = z - sign * (step - 1 if outgoing else step)
            side = y
            peer = lax.rem(z + sign + line, line) * 2 + y
        else:
            far = z - sign * step
            side = y if outgoing else 1 - y
            peer = z * 2 + 1 - y
        start = (lax.rem(far + line, line) * 2 + side) * rows
        ref = xg.at[pl.ds(pl.multiple_of(start, rows), rows), pl.ds(c * chunk, chunk)]
        index = (kind * line + step) * CHUNKS + c
        return pltpu.make_async_remote_copy(
            src_ref=ref,
            dst_ref=ref,
            send_sem=ag_send.at[index],
            recv_sem=ag_recv.at[index],
            device_id=(sec, peer),
            device_id_type=MESH,
        )

    def holds(kind, step):
        return z >= step if kind % 2 == 0 else z <= line - 1 - step

    def goes_on(kind):
        return z <= line - 2 if kind % 2 == 0 else z >= 1

    def page_copy(k):
        peer = lax.rem(me + k, n)
        return pltpu.make_async_remote_copy(
            src_ref=staged.at[k],
            dst_ref=pages.at[pl.ds(me * pool_dev, pool_dev)],
            send_sem=pg_send.at[k],
            recv_sem=pg_recv.at[k],
            device_id=(sec, peer),
            device_id_type=MESH,
        )

    def page_arrived(k):
        peer = lax.rem(me + n - k, n)
        pltpu.make_async_remote_copy(
            src_ref=staged.at[k],
            dst_ref=pages.at[pl.ds(peer * pool_dev, pool_dev)],
            send_sem=pg_send.at[k],
            recv_sem=pg_recv.at[k],
            device_id=(sec, peer),
            device_id_type=MESH,
        ).wait_recv()

    order = sorted(range(1, n), key=lambda k: (abs(k - n // 2), k))
    for c in range(CHUNKS):
        for kind in range(2):

            @pl.when(goes_on(kind))
            def _(kind=kind, c=c):
                ag_copy(kind, 1, c, True).start()

        ag_copy(2, 0, c, True).start()
    page_copies = [page_copy(k) for k in order]
    for k, copy in zip(order, page_copies):
        page_load(k).wait()
        copy.start()

    row_ids = lax.broadcasted_iota(jnp.int32, cosine.shape, 0)
    request = lax.div(row_ids, NEW)
    position = lax.rem(row_ids, NEW)
    for r in range(REQ):
        position = position + jnp.where(request == r, lens_ref[r], 0)
    even = lax.rem(lax.broadcasted_iota(jnp.int32, cosine.shape, 1), 2) == 0
    angle = position.astype(jnp.float32) * inverse_ref[...]
    cosine[...] = jnp.cos(angle)
    turned_sine = jnp.sin(angle)
    sine[...] = jnp.where(even, -turned_sine, turned_sine)

    for step in range(1, line):
        for c in range(CHUNKS):
            for kind in range(2):

                @pl.when(holds(kind, step))
                def _(kind=kind, step=step, c=c):
                    ag_copy(kind, step, c, False).wait_recv()
                    if step < line - 1:

                        @pl.when(goes_on(kind))
                        def _():
                            ag_copy(kind, step + 1, c, True).start()

                    ag_copy(kind + 2, step, c, True).start()

    tiles = q_cols // TILE
    for c in range(CHUNKS):
        part = pl.ds(c * chunk, chunk)
        ag_copy(2, 0, c, False).wait_recv()
        for step in range(1, line):
            for kind in range(2, 4):

                @pl.when(holds(kind, step))
                def _(kind=kind, step=step, c=c):
                    ag_copy(kind, step, c, False).wait_recv()

        for load in loads[c]:
            load.wait()

        def project(i, carry, c=c, part=part):
            cols = pl.ds(pl.multiple_of(i * TILE, TILE), TILE)
            term = jnp.dot(xg[:, part], wq[part, cols], preferred_element_type=jnp.float32)
            acc[:, cols] = term if c == 0 else acc[:, cols] + term
            return carry

        lax.fori_loop(0, tiles, project, 0)
        term = jnp.dot(xg[:, part], wkv[part, :], preferred_element_type=jnp.float32)
        cols = pl.ds(q_cols, pair)
        acc[:, cols] = term if c == 0 else acc[:, cols] + term

    def turn(values):
        other = jnp.where(even, pltpu.roll(values, HD - 1, 1), pltpu.roll(values, 1, 1))
        return (values * cosine[...] + other * sine[...]).astype(jnp.bfloat16)

    new_rows = REQ * NEW
    key = turn(acc[:, q_cols : q_cols + HD]).reshape(REQ, NEW, HD)
    value = acc[:, q_cols + HD : q_cols + pair].astype(jnp.bfloat16).reshape(REQ, NEW, HD)
    fresh[me, :, :, :HD] = key
    fresh[me, :, :, HD:] = value

    def fresh_copy(k, outgoing):
        peer = lax.rem(me + k, n) if outgoing else lax.rem(me + n - k, n)
        ref = fresh.at[me if outgoing else peer]
        return pltpu.make_async_remote_copy(
            src_ref=ref,
            dst_ref=ref,
            send_sem=kv_send.at[k],
            recv_sem=kv_recv.at[k],
            device_id=(sec, peer),
            device_id_type=MESH,
        )

    fresh_copies = [fresh_copy(k, True) for k in range(1, n)]
    for copy in fresh_copies:
        copy.start()
    for h in range(heads):
        turned = turn(acc[:, h * HD : (h + 1) * HD])
        qs[:, h * NEW : (h + 1) * NEW, :] = turned.reshape(REQ, NEW, HD)

    own_pages.wait()
    for k in order:
        page_arrived(k)

    kbuf[pl.ds(prefix + NEW, NEW), :] = jnp.zeros((NEW, pair), jnp.bfloat16)
    group = heads // 2
    grows = group * NEW
    prefix_column = lax.broadcasted_iota(jnp.int32, (grows, prefix), 1)
    fresh_column = lax.broadcasted_iota(jnp.int32, (grows, 2 * NEW), 1)
    token = lax.rem(lax.broadcasted_iota(jnp.int32, (grows, 2 * NEW), 0), NEW)
    causal = fresh_column <= token
    factor = HD ** (-0.5) * 1.4426950408889634
    contract = (((1,), (1,)), ((), ()))

    def one_request(r, carry):
        for j in range(listed):
            kbuf[pl.ds(j * PAGE, PAGE), :] = pages[table_ref[r * listed + j]]
        kbuf[pl.ds(prefix, NEW), :] = fresh[me, r]
        limit = lens_ref[r]
        for part in range(2):
            q = qs[r, part * grows : (part + 1) * grows, :]
            old = lax.dot_general(
                q, kbuf[:prefix, :HD], contract, preferred_element_type=jnp.float32
            )
            new = lax.dot_general(
                q, kbuf[prefix:, :HD], contract, preferred_element_type=jnp.float32
            )
            old = jnp.where(prefix_column < limit, old, -1e30)
            new = jnp.where(causal, new, -1e30)
            top = jnp.maximum(
                jnp.max(old, axis=-1, keepdims=True), jnp.max(new, axis=-1, keepdims=True)
            )
            old = jnp.exp2((old - top) * factor)
            new = jnp.exp2((new - top) * factor)
            total = jnp.sum(old, axis=-1, keepdims=True) + jnp.sum(new, axis=-1, keepdims=True)
            scale = 1.0 / total
            mixed = jnp.dot(
                (old * scale).astype(jnp.bfloat16),
                kbuf[:prefix, HD:],
                preferred_element_type=jnp.float32,
            )
            mixed = mixed + jnp.dot(
                (new * scale).astype(jnp.bfloat16),
                kbuf[prefix:, HD:],
                preferred_element_type=jnp.float32,
            )
            mixed = mixed.astype(jnp.bfloat16)
            for h in range(group):
                col = (part * group + h) * HD
                att[r, :, col : col + HD] = mixed[h * NEW : (h + 1) * NEW, :]
        return carry

    lax.fori_loop(0, REQ, one_request, 0)

    for c in range(CHUNKS):
        ag_copy(2, 0, c, True).wait_send()
        for step in range(1, line):
            for kind in range(2):

                @pl.when(holds(kind, step - 1) & goes_on(kind))
                def _(kind=kind, step=step, c=c):
                    ag_copy(kind, step, c, True).wait_send()

                @pl.when(holds(kind, step))
                def _(kind=kind, step=step, c=c):
                    ag_copy(kind + 2, step, c, True).wait_send()

    def rs_rows(offset):
        return pl.ds(pl.multiple_of(at_ring(offset) * rows, rows), rows)

    def rs_copy(direction, step, c):
        sign = 1 - 2 * direction
        index = (direction * steps + step - 1) * CHUNKS + c
        part = pl.ds(c * chunk, chunk)
        if step == 1:
            start = at_ring(sign * steps) * rows + direction * HALF
            src = xg.at[pl.ds(pl.multiple_of(start, HALF), HALF), part]
            dst = rs_half.at[direction, c]
        else:
            src = xg.at[rs_rows(sign * (steps + 1 - step)), part]
            dst = rs_full.at[direction, step - 2, c]
        return pltpu.make_async_remote_copy(
            src_ref=src,
            dst_ref=dst,
            send_sem=rs_send.at[index],
            recv_sem=rs_recv.at[index],
            device_id=(sec, at_ring(sign)),
            device_id_type=MESH,
        )

    product_tile = min(2 * TILE, chunk)
    rs_copies = {}
    for c in range(CHUNKS):
        out_loads[c].wait()

        def product(i, carry, c=c):
            cols = pl.ds(pl.multiple_of(c * chunk + i * product_tile, product_tile), product_tile)
            xg[:, cols] = jnp.dot(
                att[...].reshape(new_rows, q_cols),
                wo[:, cols],
                preferred_element_type=jnp.float32,
            ).astype(jnp.bfloat16)
            return carry

        lax.fori_loop(0, chunk // product_tile, product, 0)
        for direction in range(2):
            copy = rs_copy(direction, 1, c)
            copy.start()
            rs_copies[direction, 1, c] = copy
    for step in range(2, steps + 1):
        for c in range(CHUNKS):
            part = pl.ds(c * chunk, chunk)
            for direction in range(2):
                sign = 1 - 2 * direction
                rs_copies[direction, step - 1, c].wait_recv()
                if step == 2:
                    start = at_ring(sign * (steps - 1)) * rows + direction * HALF
                    mine = pl.ds(pl.multiple_of(start, HALF), HALF)
                    came = rs_half[direction, c]
                else:
                    mine = rs_rows(sign * (steps + 1 - step))
                    came = rs_full[direction, step - 3, c]
                xg[mine, part] = (
                    xg[mine, part].astype(jnp.float32) + came.astype(jnp.float32)
                ).astype(jnp.bfloat16)
                copy = rs_copy(direction, step, c)
                copy.start()
                rs_copies[direction, step, c] = copy

    hands = []
    own = pl.ds(pl.multiple_of(me * rows, rows), rows)
    for c in range(CHUNKS):
        part = pl.ds(c * chunk, chunk)
        for direction in range(2):
            rs_copies[direction, steps, c].wait_recv()
        summed = xg[own, part].astype(jnp.float32)
        for direction in range(2):
            summed = summed + rs_full[direction, steps - 2, c].astype(jnp.float32)
        block[:, part] = (hidden_ref[:, part].astype(jnp.float32) + summed).astype(jnp.bfloat16)
        hand = pltpu.make_async_remote_copy(
            src_ref=block.at[:, part],
            dst_ref=handed_ref.at[:, part],
            send_sem=hand_send.at[c],
            recv_sem=hand_recv.at[c],
            device_id=(next_sec, me),
            device_id_type=MESH,
        )
        hand.start()
        hands.append(hand)

    for k in range(1, n):
        fresh_copy(k, False).wait_recv()
    slots = cache_ref.shape[0]
    units = place_ref.shape[0]
    for slot in range(slots):
        wanted = me * slots + slot
        unit = jnp.int32(0)
        for u in range(units):
            unit = jnp.where(place_ref[u] == wanted, u, unit)
        cache_ref[slot] = fresh[lax.rem(unit, KVH), lax.div(unit, KVH)]

    for copy in page_copies:
        copy.wait_send()
    for copy in fresh_copies:
        copy.wait_send()
    for copy in rs_copies.values():
        copy.wait_send()
    for hand in hands:
        hand.wait()


def settle_kernel(handed_in, cache_in, handed_out, cache_out):
    handed_out[...] = handed_in[...]
    cache_out[...] = cache_in[...]


def fused(
    n,
    n_section,
    hidden,
    norm_gain,
    w_query,
    w_keyval,
    w_out,
    kv_pool,
    page_table,
    prefix_len,
    decode_place,
):
    rows, width = hidden.shape
    q_cols = w_query.shape[2]
    pool_dev = kv_pool.shape[1]
    pair = 2 * HD
    new_rows = REQ * NEW
    prefix = page_table.shape[1] // REQ * PAGE
    slots = REQ * KVH // n
    steps = n // 2
    chunk = width // CHUNKS
    heads = q_cols // HD
    lens = prefix_len[0]
    dims = jnp.arange(HD, dtype=jnp.int32)
    inverse = jnp.power(rope_theta, -(dims // 2 * 2).astype(jnp.float32) / HD)[None, :]
    vmem = pl.BlockSpec(memory_space=pltpu.VMEM)
    smem = pl.BlockSpec(memory_space=pltpu.SMEM)
    far = pl.BlockSpec(memory_space=pl.ANY)
    bf16 = jnp.bfloat16
    dma = pltpu.SemaphoreType.DMA
    handed, cache = pl.pallas_call(
        functools.partial(layer_kernel, n, n_section),
        out_shape=(
            jax.ShapeDtypeStruct((rows, width), bf16),
            jax.ShapeDtypeStruct((slots, NEW, pair), bf16),
        ),
        in_specs=[vmem, vmem, far, far, far, far, vmem, smem, smem, smem],
        out_specs=(vmem, vmem),
        scratch_shapes=[
            pltpu.VMEM((new_rows, width), bf16),
            pltpu.VMEM((width, q_cols), bf16),
            pltpu.VMEM((width, pair), bf16),
            pltpu.VMEM((q_cols, width), bf16),
            pltpu.VMEM((n * pool_dev, PAGE, pair), bf16),
            pltpu.VMEM((new_rows, q_cols + pair), jnp.float32),
            pltpu.VMEM((REQ, heads * NEW, HD), bf16),
            pltpu.VMEM((n, REQ, NEW, pair), bf16),
            pltpu.VMEM((prefix + 2 * NEW, pair), bf16),
            pltpu.VMEM((REQ, NEW, q_cols), bf16),
            pltpu.VMEM((2, CHUNKS, HALF, chunk), bf16),
            pltpu.VMEM((2, steps - 1, CHUNKS, rows, chunk), bf16),
            pltpu.VMEM((rows, width), bf16),
            pltpu.VMEM((new_rows, HD), jnp.float32),
            pltpu.VMEM((new_rows, HD), jnp.float32),
            pltpu.VMEM((n, pool_dev, PAGE, pair), bf16),
            dma((3 * CHUNKS,)),
            dma,
            dma((n,)),
            dma((4 * steps * CHUNKS,)),
            dma((4 * steps * CHUNKS,)),
            dma((n,)),
            dma((n,)),
            dma((n,)),
            dma((n,)),
            dma((2 * steps * CHUNKS,)),
            dma((2 * steps * CHUNKS,)),
            dma((CHUNKS,)),
            dma((CHUNKS,)),
        ],
        compiler_params=pltpu.CompilerParams(
            collective_id=0, has_side_effects=True, vmem_limit_bytes=60 * 1024 * 1024
        ),
        cost_estimate=pl.CostEstimate(
            flops=11_000_000_000, bytes_accessed=40_000_000, transcendentals=2_000_000
        ),
    )(
        hidden,
        norm_gain,
        w_query[0],
        w_keyval[0],
        w_out[0],
        kv_pool[0],
        inverse,
        page_table[0],
        lens,
        decode_place[0],
    )
    handed, cache = pl.pallas_call(
        settle_kernel,
        out_shape=(
            jax.ShapeDtypeStruct(handed.shape, bf16),
            jax.ShapeDtypeStruct(cache.shape, bf16),
        ),
        in_specs=[vmem, vmem],
        out_specs=(vmem, vmem),
        compiler_params=pltpu.CompilerParams(vmem_limit_bytes=60 * 1024 * 1024),
        cost_estimate=pl.CostEstimate(flops=0, bytes_accessed=1_300_000, transcendentals=0),
    )(handed, cache)
    return (handed, cache[None])


def solution(mesh):
    placed = (
        P(("section", "tp"), None),
        P("section", None),
        P("section", None, "tp"),
        P("section", None, "tp"),
        P("section", "tp", None),
        P("section", "tp", None, None),
        P("section", None),
        P("section", None),
        P("section", None),
    )
    n = mesh.shape["tp"]
    body = local
    if n == KVH:
        body = functools.partial(fused, n, mesh.shape["section"])
    return jax.shard_map(
        body,
        mesh=mesh,
        in_specs=placed,
        out_specs=(P(("section", "tp"), None), P("section", "tp", None, None)),
        check_vma=False,
    )
```

```python
import functools

import jax
import jax.numpy as jnp
from jax import lax
from jax.experimental import pallas as pl
from jax.experimental.pallas import tpu as pltpu
from jax.sharding import PartitionSpec as P

KVH = 8
HD = 128
PAGE = 128
REQ = 4
NEW = 64


rope_theta = 500000.0


def from_behind(value, axis, steps):
    count = lax.axis_size(axis)
    pairs = [(source, (source + steps) % count) for source in range(count)]
    return lax.ppermute(value, axis, pairs)


def rotate(values, positions, dims, apply, head_size):
    rows = values.shape[0]
    cols = values.shape[1]
    inverse = jnp.power(rope_theta, -(dims // 2 * 2).astype(jnp.float32) / head_size)
    angle = positions[:, None].astype(jnp.float32) * inverse[None, :]
    cosine = jnp.cos(angle)[:, 0::2]
    sine = jnp.sin(angle)[:, 0::2]
    pairs = values.reshape(rows, cols // 2, 2)
    even = pairs[:, :, 0]
    odd = pairs[:, :, 1]
    turned = jnp.stack([even * cosine - odd * sine, even * sine + odd * cosine], axis=-1).reshape(
        rows, cols
    )
    return jnp.where(apply[None, :], turned, values)


def attend(qheads, prefix_kv, fresh_kv, lens):
    prefix = prefix_kv.shape[1]
    count = qheads.shape[1]
    scale = HD ** (-0.5)
    score_pre = (
        jnp.einsum(
            "rnhd,rkd->rhnk", qheads, prefix_kv[:, :, :HD], preferred_element_type=jnp.float32
        )
        * scale
    )
    score_new = (
        jnp.einsum(
            "rnhd,rkd->rhnk", qheads, fresh_kv[:, :, :HD], preferred_element_type=jnp.float32
        )
        * scale
    )
    seen_pre = (jnp.arange(prefix, dtype=jnp.int32)[None, :] < lens[:, None])[:, None, None, :]
    npos = jnp.arange(count, dtype=jnp.int32)
    seen_new = (npos[None, :] <= npos[:, None])[None, None, :, :]
    top = jnp.maximum(
        jnp.max(jnp.where(seen_pre, score_pre, -1e30), axis=-1, keepdims=True),
        jnp.max(jnp.where(seen_new, score_new, -1e30), axis=-1, keepdims=True),
    )
    expo_pre = jnp.where(seen_pre, jnp.exp(score_pre - top), 0.0)
    expo_new = jnp.where(seen_new, jnp.exp(score_new - top), 0.0)
    total = jnp.sum(expo_pre, axis=-1, keepdims=True) + jnp.sum(expo_new, axis=-1, keepdims=True)
    weight_pre = (expo_pre / total).astype(jnp.bfloat16)
    weight_new = (expo_new / total).astype(jnp.bfloat16)
    mixed = jnp.einsum(
        "rhnk,rkd->rnhd", weight_pre, prefix_kv[:, :, HD:], preferred_element_type=jnp.float32
    )
    mixed = mixed + jnp.einsum(
        "rhnk,rkd->rnhd", weight_new, fresh_kv[:, :, HD:], preferred_element_type=jnp.float32
    )
    return mixed.astype(jnp.bfloat16)


def local(
    hidden, norm_gain, w_query, w_keyval, w_out, kv_pool, page_table, prefix_len, decode_place
):
    tp_count = lax.axis_size("tp")
    tp_rank = lax.axis_index("tp")
    w_q = w_query[0]
    w_kv = w_keyval[0]
    w_o = w_out[0]
    q_cols = w_q.shape[1]
    kv_cols = w_kv.shape[1]
    rows_dev = hidden.shape[0]
    xf = hidden.astype(jnp.float32)
    meansq = jnp.mean(xf * xf, axis=-1, keepdims=True)
    normed = (xf * lax.rsqrt(meansq + 1e-05) * norm_gain[0][None, :]).astype(jnp.bfloat16)
    project_piece = lax.all_gather(normed, "tp", axis=0, tiled=True)
    projected = jnp.concatenate(
        [
            jnp.dot(project_piece, w_q, preferred_element_type=jnp.float32),
            jnp.dot(project_piece, w_kv, preferred_element_type=jnp.float32),
        ],
        axis=1,
    )
    lens = prefix_len[0]
    positions = (lens[:, None] + jnp.arange(NEW, dtype=jnp.int32)[None, :]).reshape(-1)
    qdims = jnp.arange(q_cols, dtype=jnp.int32)
    query = rotate(projected[:, :q_cols], positions, qdims % HD, qdims >= 0, HD).astype(
        jnp.bfloat16
    )
    kdims = tp_rank * kv_cols + jnp.arange(kv_cols, dtype=jnp.int32)
    keyval = rotate(projected[:, q_cols:], positions, kdims % HD, kdims // HD % 2 == 0, HD).astype(
        jnp.bfloat16
    )
    keyval_all = lax.all_gather(keyval, "tp", axis=1, tiled=True)
    pool_local = kv_pool[0]
    pool_dev = pool_local.shape[0]
    table_flat = page_table[0]
    listed = table_flat.shape[0] // REQ
    prefix = listed * PAGE
    heads_dev = q_cols // HD
    members = tp_count // KVH
    kv_head = tp_rank // members
    by_head = pool_local.reshape(pool_dev, PAGE, KVH, 2 * HD).transpose(2, 0, 1, 3)
    outgoing = jnp.repeat(by_head, members, axis=0)
    received = lax.all_to_all(outgoing, "tp", split_axis=0, concat_axis=0, tiled=True)
    flat_pages = received.reshape(-1, PAGE, 2 * HD)
    prefix_kv = flat_pages[table_flat.reshape(REQ, listed)].reshape(REQ, prefix, 2 * HD)
    fresh_kv = lax.dynamic_slice_in_dim(keyval_all, kv_head * 2 * HD, 2 * HD, 1).reshape(
        REQ, NEW, 2 * HD
    )
    qheads = query.reshape(REQ, NEW, heads_dev, HD)
    attended = attend(qheads, prefix_kv, fresh_kv, lens).reshape(REQ * NEW, q_cols)
    summed = lax.psum(
        jnp.dot(attended, w_o, preferred_element_type=jnp.float32).astype(jnp.bfloat16), "tp"
    ).astype(jnp.float32)
    mine = lax.dynamic_slice_in_dim(summed, tp_rank * rows_dev, rows_dev, 0)
    block = (xf + mine).astype(jnp.bfloat16)
    handed = from_behind(block, "section", 1)
    slots_dev = REQ * KVH // tp_count
    places = decode_place[0]
    units = keyval_all.reshape(REQ, NEW, KVH, 2 * HD)
    unit_ids = jnp.arange(REQ * KVH, dtype=jnp.int32)
    pieces = []
    for slot in range(slots_dev):
        wanted = tp_rank * slots_dev + slot
        unit = jnp.sum(jnp.where(places == wanted, unit_ids, 0))
        request = unit // KVH
        head = unit % KVH
        zero = jnp.zeros((), jnp.int32)
        piece = lax.dynamic_slice(units, (request, zero, head, zero), (1, NEW, 1, 2 * HD))
        pieces.append(piece.reshape(NEW, 2 * HD))
    decode_cache = jnp.stack(pieces, axis=0)[None]
    return (handed, decode_cache)


MESH = pl.DeviceIdType.MESH
CHUNKS = 8
TILE = 256
HALF = 16


def ring_place(t, n):
    z, y = lax.div(t, 2), lax.rem(t, 2)
    return (1 - y) * z + y * (n - 1 - z)


def ring_member(p, n):
    half = n // 2
    far = lax.div(p, half)
    return (1 - far) * (2 * p) + far * (2 * (n - 1 - p) + 1)


def layer_kernel(
    n,
    n_section,
    hidden_ref,
    gain_ref,
    wq_hbm,
    wkv_hbm,
    wo_hbm,
    pool_hbm,
    inverse_ref,
    table_ref,
    lens_ref,
    place_ref,
    handed_ref,
    cache_ref,
    xg,
    wq,
    wkv,
    wo,
    pages,
    acc,
    qs,
    fresh,
    kbuf,
    att,
    rs_half,
    rs_full,
    block,
    cosine,
    sine,
    staged,
    w_sem,
    own_sem,
    stage_sem,
    ag_send,
    ag_recv,
    pg_send,
    pg_recv,
    kv_send,
    kv_recv,
    rs_send,
    rs_recv,
    hand_send,
    hand_recv,
):
    sec = lax.axis_index("section")
    me = lax.axis_index("tp")
    rows, width = hidden_ref.shape
    chunk = width // CHUNKS
    q_cols = wq.shape[1]
    heads = q_cols // HD
    pool_dev = pool_hbm.shape[0]
    listed = table_ref.shape[0] // REQ
    prefix = listed * PAGE
    ring = ring_place(me, n)
    next_sec = lax.rem(sec + 1, n_section)
    prev_sec = lax.rem(sec + n_section - 1, n_section)

    def at_ring(offset):
        return ring_member(lax.rem(ring + offset + 2 * n, n), n)

    barrier = pltpu.get_barrier_semaphore()
    for k in range(1, n):
        pl.semaphore_signal(
            barrier, inc=1, device_id=(sec, lax.rem(me + k, n)), device_id_type=MESH
        )
    for other in (next_sec, prev_sec):
        pl.semaphore_signal(barrier, inc=1, device_id=(other, me), device_id_type=MESH)

    pair = 2 * HD

    def page_load(k):
        peer = lax.rem(me + k, n)
        return pltpu.make_async_copy(
            pool_hbm.at[:, :, pl.ds(pl.multiple_of(peer * pair, pair), pair)],
            staged.at[k],
            stage_sem.at[k],
        )

    for k in range(1, n):
        page_load(k).start()
    loads = []
    for c in range(CHUNKS):
        part = pl.ds(c * chunk, chunk)
        first = pltpu.make_async_copy(wq_hbm.at[part, :], wq.at[part, :], w_sem.at[3 * c])
        second = pltpu.make_async_copy(wkv_hbm.at[part, :], wkv.at[part, :], w_sem.at[3 * c + 1])
        loads.append((first, second))
        first.start()
        second.start()
    out_loads = []
    for c in range(CHUNKS):
        part = pl.ds(c * chunk, chunk)
        out_loads.append(
            pltpu.make_async_copy(wo_hbm.at[:, part], wo.at[:, part], w_sem.at[3 * c + 2])
        )
        out_loads[-1].start()
    own_pages = pltpu.make_async_copy(
        pool_hbm.at[:, :, pl.ds(pl.multiple_of(me * pair, pair), pair)],
        pages.at[pl.ds(me * pool_dev, pool_dev)],
        own_sem,
    )
    own_pages.start()

    xf = hidden_ref[...].astype(jnp.float32)
    meansq = jnp.mean(xf * xf, axis=-1, keepdims=True)
    normed = (xf * lax.rsqrt(meansq + 1e-05) * gain_ref[...]).astype(jnp.bfloat16)
    xg[pl.ds(pl.multiple_of(me * rows, rows), rows), :] = normed

    pl.semaphore_wait(barrier, n - 1 + 2)

    steps = n // 2
    line = n // 2
    z, y = lax.div(me, 2), lax.rem(me, 2)

    def ag_copy(kind, step, c, outgoing):
        sign = 1 - 2 * (kind % 2)
        if kind < 2:
            far = z - sign * (step - 1 if outgoing else step)
            side = y
            peer = lax.rem(z + sign + line, line) * 2 + y
        else:
            far = z - sign * step
            side = y if outgoing else 1 - y
            peer = z * 2 + 1 - y
        start = (lax.rem(far + line, line) * 2 + side) * rows
        ref = xg.at[pl.ds(pl.multiple_of(start, rows), rows), pl.ds(c * chunk, chunk)]
        index = (kind * line + step) * CHUNKS + c
        return pltpu.make_async_remote_copy(
            src_ref=ref,
            dst_ref=ref,
            send_sem=ag_send.at[index],
            recv_sem=ag_recv.at[index],
            device_id=(sec, peer),
            device_id_type=MESH,
        )

    def holds(kind, step):
        return z >= step if kind % 2 == 0 else z <= line - 1 - step

    def goes_on(kind):
        return z <= line - 2 if kind % 2 == 0 else z >= 1

    def page_copy(k):
        peer = lax.rem(me + k, n)
        return pltpu.make_async_remote_copy(
            src_ref=staged.at[k],
            dst_ref=pages.at[pl.ds(me * pool_dev, pool_dev)],
            send_sem=pg_send.at[k],
            recv_sem=pg_recv.at[k],
            device_id=(sec, peer),
            device_id_type=MESH,
        )

    def page_arrived(k):
        peer = lax.rem(me + n - k, n)
        pltpu.make_async_remote_copy(
            src_ref=staged.at[k],
            dst_ref=pages.at[pl.ds(peer * pool_dev, pool_dev)],
            send_sem=pg_send.at[k],
            recv_sem=pg_recv.at[k],
            device_id=(sec, peer),
            device_id_type=MESH,
        ).wait_recv()

    order = sorted(range(1, n), key=lambda k: (abs(k - n // 2), k))
    for c in range(CHUNKS):
        for kind in range(2):

            @pl.when(goes_on(kind))
            def _(kind=kind, c=c):
                ag_copy(kind, 1, c, True).start()

        ag_copy(2, 0, c, True).start()
    page_copies = [page_copy(k) for k in order]
    for k, copy in zip(order, page_copies):
        page_load(k).wait()
        copy.start()

    row_ids = lax.broadcasted_iota(jnp.int32, cosine.shape, 0)
    request = lax.div(row_ids, NEW)
    position = lax.rem(row_ids, NEW)
    for r in range(REQ):
        position = position + jnp.where(request == r, lens_ref[r], 0)
    even = lax.rem(lax.broadcasted_iota(jnp.int32, cosine.shape, 1), 2) == 0
    angle = position.astype(jnp.float32) * inverse_ref[...]
    cosine[...] = jnp.cos(angle)
    turned_sine = jnp.sin(angle)
    sine[...] = jnp.where(even, -turned_sine, turned_sine)

    for step in range(1, line):
        for c in range(CHUNKS):
            for kind in range(2):

                @pl.when(holds(kind, step))
                def _(kind=kind, step=step, c=c):
                    ag_copy(kind, step, c, False).wait_recv()
                    if step < line - 1:

                        @pl.when(goes_on(kind))
                        def _():
                            ag_copy(kind, step + 1, c, True).start()

                    ag_copy(kind + 2, step, c, True).start()

    tiles = q_cols // TILE
    for c in range(CHUNKS):
        part = pl.ds(c * chunk, chunk)
        ag_copy(2, 0, c, False).wait_recv()
        for step in range(1, line):
            for kind in range(2, 4):

                @pl.when(holds(kind, step))
                def _(kind=kind, step=step, c=c):
                    ag_copy(kind, step, c, False).wait_recv()

        for load in loads[c]:
            load.wait()

        def project(i, carry, c=c, part=part):
            cols = pl.ds(pl.multiple_of(i * TILE, TILE), TILE)
            term = jnp.dot(xg[:, part], wq[part, cols], preferred_element_type=jnp.float32)
            acc[:, cols] = term if c == 0 else acc[:, cols] + term
            return carry

        lax.fori_loop(0, tiles, project, 0)
        term = jnp.dot(xg[:, part], wkv[part, :], preferred_element_type=jnp.float32)
        cols = pl.ds(q_cols, pair)
        acc[:, cols] = term if c == 0 else acc[:, cols] + term

    def turn(values):
        other = jnp.where(even, pltpu.roll(values, HD - 1, 1), pltpu.roll(values, 1, 1))
        return (values * cosine[...] + other * sine[...]).astype(jnp.bfloat16)

    new_rows = REQ * NEW
    key = turn(acc[:, q_cols : q_cols + HD]).reshape(REQ, NEW, HD)
    value = acc[:, q_cols + HD : q_cols + pair].astype(jnp.bfloat16).reshape(REQ, NEW, HD)
    fresh[me, :, :, :HD] = key
    fresh[me, :, :, HD:] = value

    def fresh_copy(k, outgoing):
        peer = lax.rem(me + k, n) if outgoing else lax.rem(me + n - k, n)
        ref = fresh.at[me if outgoing else peer]
        return pltpu.make_async_remote_copy(
            src_ref=ref,
            dst_ref=ref,
            send_sem=kv_send.at[k],
            recv_sem=kv_recv.at[k],
            device_id=(sec, peer),
            device_id_type=MESH,
        )

    fresh_copies = [fresh_copy(k, True) for k in range(1, n)]
    for copy in fresh_copies:
        copy.start()
    for h in range(heads):
        turned = turn(acc[:, h * HD : (h + 1) * HD])
        qs[:, h * NEW : (h + 1) * NEW, :] = turned.reshape(REQ, NEW, HD)

    own_pages.wait()
    for k in order:
        page_arrived(k)

    kbuf[pl.ds(prefix + NEW, NEW), :] = jnp.zeros((NEW, pair), jnp.bfloat16)
    group = heads // 2
    grows = group * NEW
    prefix_column = lax.broadcasted_iota(jnp.int32, (grows, prefix), 1)
    fresh_column = lax.broadcasted_iota(jnp.int32, (grows, 2 * NEW), 1)
    token = lax.rem(lax.broadcasted_iota(jnp.int32, (grows, 2 * NEW), 0), NEW)
    causal = fresh_column <= token
    factor = HD ** (-0.5) * 1.4426950408889634
    contract = (((1,), (1,)), ((), ()))

    def one_request(r, carry):
        for j in range(listed):
            kbuf[pl.ds(j * PAGE, PAGE), :] = pages[table_ref[r * listed + j]]
        kbuf[pl.ds(prefix, NEW), :] = fresh[me, r]
        limit = lens_ref[r]
        for part in range(2):
            q = qs[r, part * grows : (part + 1) * grows, :]
            old = lax.dot_general(
                q, kbuf[:prefix, :HD], contract, preferred_element_type=jnp.float32
            )
            new = lax.dot_general(
                q, kbuf[prefix:, :HD], contract, preferred_element_type=jnp.float32
            )
            old = jnp.where(prefix_column < limit, old, -1e30)
            new = jnp.where(causal, new, -1e30)
            top = jnp.maximum(
                jnp.max(old, axis=-1, keepdims=True), jnp.max(new, axis=-1, keepdims=True)
            )
            old = jnp.exp2((old - top) * factor)
            new = jnp.exp2((new - top) * factor)
            total = jnp.sum(old, axis=-1, keepdims=True) + jnp.sum(new, axis=-1, keepdims=True)
            scale = 1.0 / total
            mixed = jnp.dot(
                (old * scale).astype(jnp.bfloat16),
                kbuf[:prefix, HD:],
                preferred_element_type=jnp.float32,
            )
            mixed = mixed + jnp.dot(
                (new * scale).astype(jnp.bfloat16),
                kbuf[prefix:, HD:],
                preferred_element_type=jnp.float32,
            )
            mixed = mixed.astype(jnp.bfloat16)
            for h in range(group):
                col = (part * group + h) * HD
                att[r, :, col : col + HD] = mixed[h * NEW : (h + 1) * NEW, :]
        return carry

    lax.fori_loop(0, REQ, one_request, 0)

    for c in range(CHUNKS):
        ag_copy(2, 0, c, True).wait_send()
        for step in range(1, line):
            for kind in range(2):

                @pl.when(holds(kind, step - 1) & goes_on(kind))
                def _(kind=kind, step=step, c=c):
                    ag_copy(kind, step, c, True).wait_send()

                @pl.when(holds(kind, step))
                def _(kind=kind, step=step, c=c):
                    ag_copy(kind + 2, step, c, True).wait_send()

    def rs_rows(offset):
        return pl.ds(pl.multiple_of(at_ring(offset) * rows, rows), rows)

    def rs_copy(direction, step, c):
        sign = 1 - 2 * direction
        index = (direction * steps + step - 1) * CHUNKS + c
        part = pl.ds(c * chunk, chunk)
        if step == 1:
            start = at_ring(sign * steps) * rows + direction * HALF
            src = xg.at[pl.ds(pl.multiple_of(start, HALF), HALF), part]
            dst = rs_half.at[direction, c]
        else:
            src = xg.at[rs_rows(sign * (steps + 1 - step)), part]
            dst = rs_full.at[direction, step - 2, c]
        return pltpu.make_async_remote_copy(
            src_ref=src,
            dst_ref=dst,
            send_sem=rs_send.at[index],
            recv_sem=rs_recv.at[index],
            device_id=(sec, at_ring(sign)),
            device_id_type=MESH,
        )

    product_tile = min(2 * TILE, chunk)
    rs_copies = {}
    for c in range(CHUNKS):
        out_loads[c].wait()

        def product(i, carry, c=c):
            cols = pl.ds(pl.multiple_of(c * chunk + i * product_tile, product_tile), product_tile)
            xg[:, cols] = jnp.dot(
                att[...].reshape(new_rows, q_cols),
                wo[:, cols],
                preferred_element_type=jnp.float32,
            ).astype(jnp.bfloat16)
            return carry

        lax.fori_loop(0, chunk // product_tile, product, 0)
        for direction in range(2):
            copy = rs_copy(direction, 1, c)
            copy.start()
            rs_copies[direction, 1, c] = copy
    for step in range(2, steps + 1):
        for c in range(CHUNKS):
            part = pl.ds(c * chunk, chunk)
            for direction in range(2):
                sign = 1 - 2 * direction
                rs_copies[direction, step - 1, c].wait_recv()
                if step == 2:
                    start = at_ring(sign * (steps - 1)) * rows + direction * HALF
                    mine = pl.ds(pl.multiple_of(start, HALF), HALF)
                    came = rs_half[direction, c]
                else:
                    mine = rs_rows(sign * (steps + 1 - step))
                    came = rs_full[direction, step - 3, c]
                xg[mine, part] = (
                    xg[mine, part].astype(jnp.float32) + came.astype(jnp.float32)
                ).astype(jnp.bfloat16)
                copy = rs_copy(direction, step, c)
                copy.start()
                rs_copies[direction, step, c] = copy

    hands = []
    own = pl.ds(pl.multiple_of(me * rows, rows), rows)
    for c in range(CHUNKS):
        part = pl.ds(c * chunk, chunk)
        for direction in range(2):
            rs_copies[direction, steps, c].wait_recv()
        summed = xg[own, part].astype(jnp.float32)
        for direction in range(2):
            summed = summed + rs_full[direction, steps - 2, c].astype(jnp.float32)
        block[:, part] = (hidden_ref[:, part].astype(jnp.float32) + summed).astype(jnp.bfloat16)
        hand = pltpu.make_async_remote_copy(
            src_ref=block.at[:, part],
            dst_ref=handed_ref.at[:, part],
            send_sem=hand_send.at[c],
            recv_sem=hand_recv.at[c],
            device_id=(next_sec, me),
            device_id_type=MESH,
        )
        hand.start()
        hands.append(hand)

    for k in range(1, n):
        fresh_copy(k, False).wait_recv()
    slots = cache_ref.shape[0]
    units = place_ref.shape[0]
    for slot in range(slots):
        wanted = me * slots + slot
        unit = jnp.int32(0)
        for u in range(units):
            unit = jnp.where(place_ref[u] == wanted, u, unit)
        cache_ref[slot] = fresh[lax.rem(unit, KVH), lax.div(unit, KVH)]

    for copy in page_copies:
        copy.wait_send()
    for copy in fresh_copies:
        copy.wait_send()
    for copy in rs_copies.values():
        copy.wait_send()
    for hand in hands:
        hand.wait()


def settle_kernel(handed_in, cache_in, handed_out, cache_out):
    handed_out[...] = handed_in[...]
    cache_out[...] = cache_in[...]


def fused(
    n,
    n_section,
    hidden,
    norm_gain,
    w_query,
    w_keyval,
    w_out,
    kv_pool,
    page_table,
    prefix_len,
    decode_place,
):
    rows, width = hidden.shape
    q_cols = w_query.shape[2]
    pool_dev = kv_pool.shape[1]
    pair = 2 * HD
    new_rows = REQ * NEW
    prefix = page_table.shape[1] // REQ * PAGE
    slots = REQ * KVH // n
    steps = n // 2
    chunk = width // CHUNKS
    heads = q_cols // HD
    lens = prefix_len[0]
    dims = jnp.arange(HD, dtype=jnp.int32)
    inverse = jnp.power(rope_theta, -(dims // 2 * 2).astype(jnp.float32) / HD)[None, :]
    vmem = pl.BlockSpec(memory_space=pltpu.VMEM)
    smem = pl.BlockSpec(memory_space=pltpu.SMEM)
    far = pl.BlockSpec(memory_space=pl.ANY)
    bf16 = jnp.bfloat16
    dma = pltpu.SemaphoreType.DMA
    handed, cache = pl.pallas_call(
        functools.partial(layer_kernel, n, n_section),
        out_shape=(
            jax.ShapeDtypeStruct((rows, width), bf16),
            jax.ShapeDtypeStruct((slots, NEW, pair), bf16),
        ),
        in_specs=[vmem, vmem, far, far, far, far, vmem, smem, smem, smem],
        out_specs=(vmem, vmem),
        scratch_shapes=[
            pltpu.VMEM((new_rows, width), bf16),
            pltpu.VMEM((width, q_cols), bf16),
            pltpu.VMEM((width, pair), bf16),
            pltpu.VMEM((q_cols, width), bf16),
            pltpu.VMEM((n * pool_dev, PAGE, pair), bf16),
            pltpu.VMEM((new_rows, q_cols + pair), jnp.float32),
            pltpu.VMEM((REQ, heads * NEW, HD), bf16),
            pltpu.VMEM((n, REQ, NEW, pair), bf16),
            pltpu.VMEM((prefix + 2 * NEW, pair), bf16),
            pltpu.VMEM((REQ, NEW, q_cols), bf16),
            pltpu.VMEM((2, CHUNKS, HALF, chunk), bf16),
            pltpu.VMEM((2, steps - 1, CHUNKS, rows, chunk), bf16),
            pltpu.VMEM((rows, width), bf16),
            pltpu.VMEM((new_rows, HD), jnp.float32),
            pltpu.VMEM((new_rows, HD), jnp.float32),
            pltpu.VMEM((n, pool_dev, PAGE, pair), bf16),
            dma((3 * CHUNKS,)),
            dma,
            dma((n,)),
            dma((4 * steps * CHUNKS,)),
            dma((4 * steps * CHUNKS,)),
            dma((n,)),
            dma((n,)),
            dma((n,)),
            dma((n,)),
            dma((2 * steps * CHUNKS,)),
            dma((2 * steps * CHUNKS,)),
            dma((CHUNKS,)),
            dma((CHUNKS,)),
        ],
        compiler_params=pltpu.CompilerParams(
            collective_id=0, has_side_effects=True, vmem_limit_bytes=60 * 1024 * 1024
        ),
        cost_estimate=pl.CostEstimate(
            flops=11_000_000_000, bytes_accessed=40_000_000, transcendentals=2_000_000
        ),
    )(
        hidden,
        norm_gain,
        w_query[0],
        w_keyval[0],
        w_out[0],
        kv_pool[0],
        inverse,
        page_table[0],
        lens,
        decode_place[0],
    )
    handed, cache = pl.pallas_call(
        settle_kernel,
        out_shape=(
            jax.ShapeDtypeStruct(handed.shape, bf16),
            jax.ShapeDtypeStruct(cache.shape, bf16),
        ),
        in_specs=[vmem, vmem],
        out_specs=(vmem, vmem),
        compiler_params=pltpu.CompilerParams(vmem_limit_bytes=60 * 1024 * 1024),
        cost_estimate=pl.CostEstimate(flops=0, bytes_accessed=1_300_000, transcendentals=0),
    )(handed, cache)
    return (handed, cache[None])


def solution(mesh):
    placed = (
        P(("section", "tp"), None),
        P("section", None),
        P("section", None, "tp"),
        P("section", None, "tp"),
        P("section", "tp", None),
        P("section", "tp", None, None),
        P("section", None),
        P("section", None),
        P("section", None),
    )
    n = mesh.shape["tp"]
    body = local
    if n == KVH:
        body = functools.partial(fused, n, mesh.shape["section"])
    return jax.shard_map(
        body,
        mesh=mesh,
        in_specs=placed,
        out_specs=(P(("section", "tp"), None), P("section", "tp", None, None)),
        check_vma=False,
    )
```
